32 devices in a mesh: dp: 16 (over z, y, x), mp: 2 (over core).
Axes of the slice: x: 2, y: 2, z: 4, core: 2. Of those that a mesh axis runs over, the one named last changes fastest.
Arguments:
- inputs: float32 [32768, 512], P(('dp', 'mp')), may hold values from -6 to 6
- segment_ids: int32 [32, 1024], P('dp'), may hold values from 0 to 3, never falling along the last dimension, each value on 1 to 512 neighbouring positions
- first_gain: float32 [512], replicated, may hold values from 0.5 to 1.5
- first_shift: float32 [512], replicated, may hold values from -3 to 3
- qkv_weight: float32 [3, 512, 512], P(None, None, 'mp'), may hold values from -0.25 to 0.25
- out_weight: float32 [512, 512], P('mp'), may hold values from -1 to 1
- features: float32 [8, 256, 64], P('mp'), may hold values from -4 to 4
- second_gain: float32 [512], replicated, may hold values from 0.5 to 1.5
- second_shift: float32 [512], replicated, may hold values from -3 to 3
- in_weight: float32 [512, 2048], P(None, 'mp'), may hold values from -0.25 to 0.25
- in_bias: float32 [2048], P('mp'), may hold values from -3 to 3
- back_weight: float32 [2048, 512], P('mp'), may hold values from -0.125 to 0.125
- back_bias: float32 [512], replicated, may hold values from -3 to 3
- cotangent: float32 [32768, 512], P(('dp', 'mp')), may hold values from -6 to 6
Outputs:
- output: float32 [32768, 512], P(('dp', 'mp'))
- g_inputs: float32 [32768, 512], P(('dp', 'mp'))
- g_first_gain: float32 [512], replicated
- g_first_shift: float32 [512], replicated
- g_qkv_weight: float32 [3, 512, 512], P(None, None, 'mp')
- g_out_weight: float32 [512, 512], P('mp')
- g_second_gain: float32 [512], replicated
- g_second_shift: float32 [512], replicated
- input_weight_gradient: float32 [512, 2048], P(None, 'mp')
- g_in_bias: float32 [2048], P('mp')
- g_back_weight: float32 [2048, 512], P('mp')
- g_back_bias: float32 [512], replicated
The draws below stay inside these ranges and needn't reach their ends.
Inputs may be any that keep to these rules, and one draw needn't show every extreme that they name: `segment_ids`: along each row the ids never fall and start at 0; each of the 4 proteins of a row has 1 to 512 tokens, one exactly 512.
All inputs are finite; a program needn't handle non-finite values.
Results may differ from the reference program's by a relative error of at most 0.0003.
Values sent between devices are 32-bit elements; how exact they have to be, the bound alone decides.
A program may use at most 320 MiB of HBM per device.

```python
import math
from functools import partial
import jax
import jax.numpy as jnp
import numpy as np
from jax import lax

D = 512
H = 8
HD = 64
M = 256
FF = 2048
ROW_LEN = 1024
SEGS = 4
PROT_MAX = 512
SEQS = 32
TOKENS = 32768


def level_of(own_key, extent, shards, smallest, largest):
    def one(dim, shards_of):
        heights = jax.random.uniform(jax.random.fold_in(jax.random.fold_in(own_key, 6), dim), (shards_of,), jnp.float32, smallest / len(shards), largest / len(shards))
        return jnp.repeat(jnp.exp(heights), extent[dim] // shards_of).reshape((-1,) + (1,) * (len(extent) - dim - 1))

    level = one(*shards[0])
    for cut in shards[1:]:
        level = level * one(*cut)
    return level


def profile(number_of, total, most, lean):
    loads = [(1 << 20) // math.isqrt(standing ** lean) + 1 for standing in range(2, number_of + 1)]
    rest, counts = total - most - (number_of - 1), [1] * (number_of - 1)
    while rest > 0:
        free = [i for i in range(number_of - 1) if counts[i] < most]
        mass, left = sum([loads[i] for i in free]), rest
        for i in free:
            extra = min(most - counts[i], max(1, left * loads[i] // mass), rest)
            counts[i] = counts[i] + extra
            rest = rest - extra
    return np.array([most] + counts)


def uneven(own_key, count, total, reach, slope):
    if count == 2:
        one = jax.random.randint(own_key, (), max(1, total - reach), min(reach, total - 1) + 1)
        return jnp.stack([one, total - one])
    lengths = jnp.asarray(profile(count, total, reach, slope), jnp.int32)
    couples = (count - 1) // 2
    source_of, receiver = lengths[1:1 + 2 * couples:2], lengths[2:2 + 2 * couples:2]
    margin = jnp.minimum(source_of - 1, reach - receiver)
    moved = jax.random.randint(jax.random.fold_in(own_key, 1), (couples,), 0, 1 << 20) % (margin + 1)
    lengths = lengths.at[1:1 + 2 * couples:2].set(source_of - moved).at[2:2 + 2 * couples:2].set(receiver + moved)
    return lengths[jax.random.permutation(jax.random.fold_in(own_key, 2), count)]


def scatter_about(key, shape, width, bound, split=(), kind=jnp.bfloat16):
    result = width * jax.random.normal(key, shape, jnp.float32)
    if split:
        result = result * level_of(key, shape, split, -0.22, 0.18)
    return jnp.clip(result, -bound, bound).astype(kind)


def setup_inputs(seed: int = 0) -> dict:
    key_list = jax.random.split(jax.random.key(seed), 15)
    inputs = scatter_about(key_list[0], (TOKENS, D), 1.0, 6.0, ((0, 32),), jnp.float32)
    segment_ids = jax.vmap(lambda own: jnp.searchsorted(jnp.cumsum(uneven(own, SEGS, ROW_LEN, PROT_MAX, 2)), jnp.arange(ROW_LEN), side="right"))(jax.random.split(key_list[1], SEQS)).reshape((SEQS, ROW_LEN)).astype(jnp.int32)
    first_gain = jnp.clip(1.0 + 0.1 * jax.random.normal(key_list[2], (D,), jnp.float32), 0.5, 1.5)
    first_shift = scatter_about(key_list[3], (D,), 0.3, 3.0, (), jnp.float32)
    qkv_weight = scatter_about(key_list[4], (3, D, H * HD), D ** -0.5, 0.25, ((2, 2),), jnp.float32)
    out_weight = scatter_about(key_list[5], (H * HD, D), (H * HD // 16) ** -0.5, 1.0, ((0, 2),), jnp.float32)
    features = scatter_about(key_list[6], (H, M, HD), 1.0, 4.0, ((0, 2),), jnp.float32)
    second_gain = jnp.clip(1.0 + 0.1 * jax.random.normal(key_list[7], (D,), jnp.float32), 0.5, 1.5)
    second_shift = scatter_about(key_list[8], (D,), 0.3, 3.0, (), jnp.float32)
    in_weight = scatter_about(key_list[9], (D, FF), D ** -0.5, 0.25, ((1, 2),), jnp.float32)
    in_bias = scatter_about(key_list[10], (FF,), 0.3, 3.0, ((0, 2),), jnp.float32)
    back_weight = scatter_about(key_list[11], (FF, D), FF ** -0.5, 0.125, ((0, 2),), jnp.float32)
    back_bias = scatter_about(key_list[12], (D,), 0.3, 3.0, (), jnp.float32)
    cotangent = scatter_about(key_list[13], (TOKENS, D), 1.0, 6.0, ((0, 32),), jnp.float32)
    return {"inputs": inputs, "segment_ids": segment_ids, "first_gain": first_gain, "first_shift": first_shift, "qkv_weight": qkv_weight, "out_weight": out_weight, "features": features, "second_gain": second_gain, "second_shift": second_shift, "in_weight": in_weight, "in_bias": in_bias, "back_weight": back_weight, "back_bias": back_bias, "cotangent": cotangent}


epsilon = 1e-05
top_precision = lax.Precision.HIGHEST

def layer_norm(vector, gain, shift):
    average = lax.optimization_barrier(jnp.mean(vector, -1, keepdims=True))
    centred = vector - average
    spread = lax.optimization_barrier(jnp.mean(centred * centred, -1, keepdims=True))
    return centred * lax.rsqrt(spread + epsilon) * gain + shift

def feature_map(vector, features):
    scaled_values = vector * vector.shape[-1] ** (-0.25)
    project_rows = jnp.einsum('wer,esr->wes', scaled_values, features, precision=top_precision)
    return jnp.exp(project_rows - 0.5 * lax.optimization_barrier(jnp.sum(scaled_values * scaled_values, -1, keepdims=True))) * features.shape[1] ** (-0.5)

def row_attend(pieces, features):
    queries, keyset, values_in, seg_row = pieces
    query_feats = feature_map(queries, features)
    key_feats = feature_map(keyset, features)
    length = seg_row.shape[0]
    causal = jnp.tril(jnp.ones((length, length), jnp.float32))
    allowed = causal * (seg_row[:, None] == seg_row[None, :]).astype(jnp.float32)
    scores = jnp.einsum('ihm,jhm->hij', query_feats, key_feats, precision=top_precision) * allowed[None]
    weighted = jnp.einsum('hij,jhd->ihd', scores, values_in, precision=top_precision)
    totals = jnp.transpose(lax.optimization_barrier(jnp.sum(scores, -1)))
    return weighted / totals[:, :, None]

def forward(features, segment_ids, inputs, first_gain, first_shift, qkv_weight, out_weight, second_gain, second_shift, in_weight, in_bias, back_weight, back_bias):
    count_of_rows, length = segment_ids.shape
    head_count, _, head_size = features.shape
    first_normed = layer_norm(inputs, first_gain, first_shift)
    project_rows = jnp.einsum('nd,cde->cne', first_normed, qkv_weight, precision=top_precision)
    project_rows = project_rows.reshape(3, count_of_rows, length, head_count, head_size)
    attend = jax.checkpoint(partial(row_attend, features=features))
    mixed = lax.map(attend, (project_rows[0], project_rows[1], project_rows[2], segment_ids))
    mixed = mixed.reshape(count_of_rows * length, head_count * head_size)
    middle = inputs + jnp.dot(mixed, out_weight, precision=top_precision)
    second_normed = layer_norm(middle, second_gain, second_shift)
    hidden = jax.nn.gelu(jnp.dot(second_normed, in_weight, precision=top_precision) + in_bias)
    return middle + jnp.dot(hidden, back_weight, precision=top_precision) + back_bias

def reference(inputs, segment_ids, first_gain, first_shift, qkv_weight, out_weight, features, second_gain, second_shift, in_weight, in_bias, back_weight, back_bias, cotangent):
    output, backward = jax.vjp(partial(forward, features, segment_ids), inputs, first_gain, first_shift, qkv_weight, out_weight, second_gain, second_shift, in_weight, in_bias, back_weight, back_bias)
    grads = backward(cotangent)
    return (output, grads[0], grads[1], grads[2], grads[3], grads[4], grads[5], grads[6], grads[7], grads[8], grads[9], grads[10])
```

```python
import functools
import math

import jax
import jax.numpy as jnp
from jax import lax
from jax.experimental import pallas as pl
from jax.experimental.pallas import tpu as pltpu
from jax.sharding import PartitionSpec as P

f32 = jnp.float32
bf16 = jnp.bfloat16
EPS = 1e-05
C = 256
BH = 256
VMEM_LIMIT = 60 * 1024 * 1024
MESH = pl.DeviceIdType.MESH
NN = (((1,), (0,)), ((), ()))
NT = (((1,), (1,)), ((), ()))
TN = (((0,), (0,)), ((), ()))


def split(x):
    hi = x.astype(bf16)
    return hi, (x - hi.astype(f32)).astype(bf16)


def dot(a, b, dims=NN):
    return lax.dot_general(a, b, dims, preferred_element_type=f32)


def dot3(a, b, dims=NN):
    left, right = dims[0][0][0], dims[0][1][0]
    return dot(jnp.concatenate([a[0], a[0], a[1]], left), jnp.concatenate([b[0], b[1], b[0]], right), dims)


def stats(v):
    mean = jnp.mean(v, -1, keepdims=True)
    centred = v - mean
    rs = lax.rsqrt(jnp.mean(centred * centred, -1, keepdims=True) + EPS)
    return centred * rs, rs


def lanes(n):
    return lax.broadcasted_iota(jnp.int32, (n, 128), 1)


def half_split(x):
    hi = x.astype(bf16).astype(f32)
    return hi, x - hi


def swap_halves(x):
    return pltpu.roll(x, 64, 1)


def pack(first, second):
    return jnp.concatenate([first.astype(bf16), second.astype(bf16)], 1)


def left_pack(x, extra, lane):
    hi, lo = half_split(x)
    hi_turned = swap_halves(hi)
    return (
        pack(jnp.where(lane < 64, hi, swap_halves(lo)), jnp.where(lane < 64, hi, extra)),
        pack(jnp.where(lane < 64, hi_turned, lo), jnp.where(lane < 64, hi_turned, extra)),
    )


def right_pack(x, extras, lane):
    hi, lo = half_split(x)
    hi_turned = swap_halves(hi)

    def second(low, e):
        e_hi, e_lo = half_split(e)
        return jnp.where(lane < 64, low, jnp.where(lane < 66, e_hi, jnp.where(lane == 66, e_lo, 0.0)))

    return (
        pack(jnp.where(lane < 64, hi, hi_turned), second(lo, extras[0])),
        pack(jnp.where(lane < 64, hi_turned, hi), second(swap_halves(lo), extras[1])),
    )


def stack_rows(x, order):
    halves = half_split(x)
    row = lax.broadcasted_iota(jnp.int32, (16, x.shape[1]), 0)
    last = jnp.zeros((16, x.shape[1]), f32)
    for i, which in enumerate(order):
        last = jnp.where(row == i, halves[which][64:65], last)
    blocks = [halves[which][:64] for which in order] + [last, jnp.zeros((48, x.shape[1]), f32)]
    return jnp.concatenate(blocks, 0).astype(bf16)


def wide(x):
    hi, lo = split(x)
    return jnp.concatenate([hi, lo], 1)


def fold(x):
    return x[:, :128] + x[:, 128:]


def with_row(x, row, at):
    place = lax.broadcasted_iota(jnp.int32, (16, x.shape[1]), 0)
    return jnp.concatenate([x, jnp.where(place == at, row, 0.0)], 0)


def make_masks(masks, segc, segr, segs):
    ids = segs[pl.ds(lax.axis_index("mp"), 1), :].astype(f32)
    segr[...] = ids
    for c in range(segc.shape[0] // C):
        segc[c * C : (c + 1) * C, :] = jnp.broadcast_to(ids[:, c * C : (c + 1) * C], (128, C)).T
    row = lax.broadcasted_iota(jnp.int32, (C, C), 0)
    col = lax.broadcasted_iota(jnp.int32, (C, C), 1)
    for c in range(segc.shape[0] // C):
        same = segc[c * C : (c + 1) * C, 0:1] == segr[:, c * C : (c + 1) * C]
        masks[c] = jnp.where(same & (row >= col), 1.0, 0.0)


def seg_flags(segc, segr, c):
    rows, row = segc[c * C : (c + 1) * C, 0:1], segr[:, c * C : (c + 1) * C]
    last = segc[(c + 1) * C - 1 : (c + 1) * C, 0:1]
    tail = ((rows == last).astype(f32), (row == last).astype(f32))
    if c == 0:
        return None, tail, None
    before = segc[c * C - 1 : c * C, 0:1]
    return ((rows == before).astype(f32), (row == before).astype(f32)), tail, (last == before).astype(f32)


def attn_fwd(
    x, gain, shift, segs, w, features,
    sq, sk, vv, qfh, qfl, kfh, kfl, ah, al, sp, mixed, invt, fback, wh, wl,
    qs, ks, vs, n1h, n1l, masks, segc, segr, wv, fv, load, mp_ss, mp_rs,
):
    step = pl.program_id(0)
    side = step // 2
    pair = step % 2
    tokens = x.shape[0]
    chunks = tokens // C
    scale = 64.0 ** -0.25
    other = {"mp": 1 - lax.axis_index("mp")}
    swaps = [
        pltpu.make_async_remote_copy(
            src_ref=ref.at[0], dst_ref=ref.at[1], send_sem=mp_ss.at[i], recv_sem=mp_rs.at[i], device_id=other, device_id_type=MESH
        )
        for i, ref in enumerate((wv, fv))
    ]

    def project(which):
        ws = [split(wv[which, i]) for i in range(3)]
        for c in range(chunks):
            rows = pl.ds(c * C, C)
            n1 = (n1h[rows, :], n1l[rows, :])
            qs[rows, :] = dot3(n1, ws[0]) * scale
            ks[rows, :] = dot3(n1, ws[1]) * scale
            vs[rows, :] = dot3(n1, ws[2])

    @pl.when(step == 0)
    def _():
        own = [pltpu.make_async_copy(src, dst.at[0], load.at[i]) for i, (src, dst) in enumerate(((w, wv), (features, fv)))]
        for copy in own:
            copy.start()
        barrier = pltpu.get_barrier_semaphore()
        pl.semaphore_signal(barrier, inc=1, device_id=other, device_id_type=MESH)
        for c in range(chunks):
            rows = pl.ds(c * C, C)
            n, _ = stats(x[rows, :])
            n1h[rows, :], n1l[rows, :] = split(n * gain[...] + shift[...])
        make_masks(masks, segc, segr, segs)
        for copy in own:
            copy.wait()
        pl.semaphore_wait(barrier, 1)
        for copy in swaps:
            copy.start()
        project(0)

    @pl.when(step == 2)
    def _():
        for copy in swaps:
            copy.wait()
        project(1)

    at = pl.ds(pl.multiple_of(pair * 128, 128), 128)
    for i in range(3):
        wh[i], wl[i] = split(wv[side, i, :, at])
    lane = lanes(C)
    m = features.shape[2]
    ones = jnp.where(lane == 64, 1.0, 0.0)
    fright = []
    for h in range(2):
        fhi, flo = half_split(fv[side, pair * 2 + h])
        gap = jnp.zeros_like(fhi)
        fright.append(jnp.concatenate([fhi, fhi, flo, gap], 0).astype(bf16))
        fback[h] = jnp.concatenate([gap, fhi, gap, flo] if h else [fhi, gap, flo, gap], 0).astype(bf16)

    def feats(s):
        squares = s * s
        left = left_pack(s, 0.0, lane)
        out = []
        for h in range(2):
            half = 0.5 * jnp.sum(jnp.where(lane // 64 == h, squares, 0.0), -1, keepdims=True) + 0.5 * math.log(m)
            out.append(split(jnp.exp(dot(left[h], fright[h]) - half)))
        return out

    state = [None, None]
    for c in range(chunks):
        rows = pl.ds(c * C, C)
        q, k, v = qs[rows, at], ks[rows, at], vs[rows, at]
        sq[rows, :] = q
        sk[rows, :] = k
        vv[rows, :] = v
        qf = feats(q)
        kf = feats(k)
        cont, tail, carry = seg_flags(segc, segr, c)
        vt = v.T
        nums = []
        for h in range(2):
            qfh[h, rows, :], qfl[h, rows, :] = qf[h]
            kfh[h, rows, :], kfl[h, rows, :] = kf[h]
            va = wide(jnp.where(lane < 64, swap_halves(v) if h else v, ones))
            a = split(dot3(qf[h], kf[h], NT) * masks[c])
            ah[h, rows, :], al[h, rows, :] = a
            num = fold(dot(a[0], va)) + dot(a[1], va[:, :128])
            if c > 0:
                hi, lo = split(state[h])
                gap = jnp.zeros((48, m), bf16)
                both = jnp.concatenate([hi, gap, lo, gap], 0)
                num = num + cont[0] * (fold(dot(qf[h][0], both, NT)) + dot(qf[h][1], both[:128], NT))
            if c < chunks - 1:
                vat = with_row(vt[h * 64 : (h + 1) * 64], 1.0, 0)
                fresh = dot3(split(vat * tail[1]), kf[h])
                state[h] = fresh if c == 0 else fresh + carry * state[h]
                sp[h, c] = stack_rows(state[h], (0, 1, 0))
            nums.append(num)
        inv = [1.0 / num[:, 64:65] for num in nums]
        mixed[rows, :] = jnp.where(lane < 64, nums[0] * inv[0], swap_halves(nums[1] * inv[1]))
        invt[rows, :] = jnp.where(lane < 64, inv[0], inv[1])


def flat_put(flat, start, value):
    tiles = value.shape[0] // 8
    for j in range(value.shape[1] // 128):
        flat[start + j * tiles : start + (j + 1) * tiles] = value[:, j * 128 : (j + 1) * 128].reshape(tiles, 8, 128)


def wout_rows(wout_s, wout_o):
    s, o = wout_s[...], wout_o[...]
    parts = [w[i : i + 128] for i in range(0, s.shape[0], 128) for w in (s, o)]
    return split(jnp.concatenate(parts, 0))


class Sum:
    def __init__(self, total, landed, done, send, recv, me, bits, polls, first=0, last=8):
        self.total, self.landed, self.done = total, landed, done
        self.send, self.recv, self.me, self.bits, self.polls = send, recv, me, bits, polls
        self.first, self.last = first * 2 * bits // 8, last * 2 * bits // 8
        units = done.shape[0] >> bits
        self.parts = []
        base = 0
        for i in range(3):
            n = ((units * (i + 1)) // 3 - (units * i) // 3) << bits
            if n:
                turn = [0, (bits + 1) // 4, (bits + 1) * 2 // 4][i]
                low = list(range(bits - 1))
                self.parts.append((base, n, low[turn:] + low[:turn] + [bits - 1], i))
            base += n

    def offset(self, part, step):
        base, n, order, _ = part
        for k in range(step):
            base = base + ((self.me >> order[k]) & 1) * (n >> (k + 1))
        return base

    def halving(self, part, step):
        base, n, order, i = part
        half = n >> (step + 1)
        mine = (self.me >> order[step]) & 1
        return pltpu.make_async_remote_copy(
            src_ref=self.total.at[pl.ds(self.offset(part, step) + (1 - mine) * half, half)],
            dst_ref=self.landed.at[pl.ds(base + n - (n >> step), half)],
            send_sem=self.send.at[i, step],
            recv_sem=self.recv.at[i, step],
            device_id={"dp": self.me ^ (1 << order[step])},
            device_id_type=MESH,
        )

    def add(self, part, step):
        base, n, order, _ = part
        half = n >> (step + 1)
        mine = (self.me >> order[step]) & 1
        keep = pl.ds(self.offset(part, step) + mine * half, half)
        to = self.done if step == self.bits - 1 else self.total
        to[keep] = self.total[keep] + self.landed[pl.ds(base + n - (n >> step), half)]

    def doubling(self, part, step):
        _, n, order, i = part
        at = pl.ds(self.offset(part, step + 1), n >> (step + 1))
        return pltpu.make_async_remote_copy(
            src_ref=self.done.at[at],
            dst_ref=self.done.at[at],
            send_sem=self.send.at[i, self.bits + step],
            recv_sem=self.recv.at[i, self.bits + step],
            device_id={"dp": self.me ^ (1 << order[step])},
            device_id_type=MESH,
        )

    def event(self, part, k):
        bits = self.bits
        end, begin = k > self.first, k < self.last
        if end and 0 < k <= bits:
            self.halving(part, k - 1).wait()
            self.add(part, k - 1)
        if end and k > bits:
            self.doubling(part, 2 * bits - k).wait()
        if begin and k < bits:
            self.halving(part, k).start()
        elif begin and k < 2 * bits:
            self.doubling(part, 2 * bits - k - 1).start()

    def due(self, q):
        todo = []
        for k in range(self.first, self.last + 1):
            at = self.polls[min(8, (k * 8 + 2 * self.bits - 1) // (2 * self.bits))]
            if at == q:
                todo += [(self, p, k) for p in self.parts]
        return todo


def greet(dp, flips, other):
    barrier = pltpu.get_barrier_semaphore()
    for flip in flips:
        pl.semaphore_signal(barrier, inc=1, device_id={"dp": dp ^ flip}, device_id_type=MESH)
    pl.semaphore_signal(barrier, inc=1, device_id=other, device_id_type=MESH)
    pl.semaphore_wait(barrier, len(flips) + 1)


def unpack(flat, start, shape, out, sem):
    tiles = shape[0] // 8
    return [
        pltpu.make_async_copy(
            flat.at[start + j * tiles : start + (j + 1) * tiles].reshape(shape[0], 128), out.at[:, j * 128 : (j + 1) * 128], sem.at[j]
        )
        for j in range(shape[1] // 128)
    ]


FFN_POLLS = (
    [6, 9, 11, 13, 15, 17, 19, 21, 24],
    [12, 15, 17, 19, 21, 24, 25],
    [18, 21, 23, 24, 25],
    [24, 25],
)
FFN_LAST = (8, 6, 4, 1)


def ffn(
    bits,
    wout_s, wout_o, gain, shift, back_bias, win_s, bin_s, wback_s, win_o, bin_o, wback_o,
    x, mixed, cot,
    out, gmid, gmix, gout, smalls, gback0, gin0, sums_left,
    mixv, cotv, middle, acc, gacc, n2h, n2l, coth, cotl, hh, hl, ph, plo,
    both, arrived, landed, done, gbin,
    load, store, mp_ss, mp_rs, ss, rs,
):
    i = pl.program_id(0)
    steps = pl.num_programs(0)
    tokens, d = x.shape
    dp = lax.axis_index("dp")
    other = {"mp": 1 - lax.axis_index("mp")}
    theirs, mine = both.at[0], both.at[1]
    groups = both.shape[1]
    sums = [
        Sum(mine.at[j], landed.at[j], done.at[j], ss.at[j], rs.at[j], dp, bits, FFN_POLLS[j], 0, FFN_LAST[j])
        for j in range(groups)
    ]

    def swap(j):
        return pltpu.make_async_remote_copy(
            src_ref=theirs.at[j], dst_ref=arrived.at[j], send_sem=mp_ss.at[j], recv_sem=mp_rs.at[j],
            device_id=other, device_id_type=MESH,
        )

    def join(j):
        swap(j).wait()
        both[1, j] = both[1, j] + arrived[j]

    def poll(q_in_step):
        for step in range(8):
            q = 3 * step + q_in_step
            todo = [e for one in sums for e in one.due(q)]
            if not todo:
                continue

            @pl.when(i == step)
            def _():
                run(todo)

    def run(todo):
        for one, p, k in todo:
            if k == 0 and p is one.parts[0]:
                join(sums.index(one))
            one.event(p, k)

    @pl.when(i == 0)
    def _():
        loads = [
            [
                pltpu.make_async_copy(src.at[t * C : (t + 1) * C], dst.at[t * C : (t + 1) * C], load.at[k, t])
                for k, (src, dst) in enumerate(((x, acc), (mixed, mixv), (cot, cotv)))
            ]
            for t in range(tokens // C)
        ]
        for copies in loads:
            for copy in copies:
                copy.start()
        greet(dp, [1 << b for b in range(bits)], other)
        wo = wout_rows(wout_s, wout_o)
        for t in range(tokens // C):
            for copy in loads[t]:
                copy.wait()
            rows = pl.ds(t * C, C)
            mid = acc[rows, :] + dot3(split(mixv[rows, :]), wo)
            middle[rows, :] = mid
            n, _ = stats(mid)
            n2h[rows, :], n2l[rows, :] = split(n * gain[...] + shift[...])
            coth[rows, :], cotl[rows, :] = split(cotv[rows, :])
            acc[rows, :] = jnp.zeros_like(mid)
            gacc[rows, :] = jnp.zeros_like(mid)

    poll(0)
    bias = jnp.where(i % 2 == 0, bin_s[...], bin_o[...])
    wi = split(jnp.where(i % 2 == 0, win_s[...], win_o[...]))
    wb = split(jnp.where(i % 2 == 0, wback_s[...], wback_o[...]))
    c0 = 0.7978845608028654
    gb = jnp.zeros((1, BH), f32)
    for t in range(tokens // C):
        if t == tokens // C // 2:
            poll(1)
        rows = pl.ds(t * C, C)
        n2 = (n2h[rows, :], n2l[rows, :])
        ct = (coth[rows, :], cotl[rows, :])
        u = dot3(n2, wi) + bias
        gh = dot3(ct, wb, NT)
        u2 = u * u
        th = jnp.tanh(c0 * (u + 0.044715 * (u2 * u)))
        hid = split(0.5 * u * (1.0 + th))
        slope = 0.5 * (1.0 + th) + 0.5 * u * (1.0 - th * th) * (c0 * (1.0 + 0.134145 * u2))
        gp = gh * slope
        gb = gb + jnp.sum(gp, 0, keepdims=True)
        gpre = split(gp)
        hh[rows, :], hl[rows, :] = hid
        ph[rows, :], plo[rows, :] = gpre
        acc[rows, :] = acc[rows, :] + dot3(hid, wb)
        gacc[rows, :] = gacc[rows, :] + dot3(gpre, wi, NT)
    gbin[pl.ds(i, 1), :] = gb
    poll(2)
    j = i // 2
    flat = both.at[i % 2, j]
    for m in range(d // C):
        cols = pl.ds(m * C, C)
        flat_put(flat, m * BH * C // 1024, dot3((hh[...], hl[...]), (coth[:, cols], cotl[:, cols]), TN))
    for m in range(BH // C):
        cols = pl.ds(m * C, C)
        flat_put(flat, d * BH // 1024 + m * d * C // 1024, dot3((n2h[...], n2l[...]), (ph[:, cols], plo[:, cols]), TN))

    @pl.when(i % 2 == 0)
    def _():
        swap(j).start()

    @pl.when(i == steps - 1)
    def _():
        run([e for one in sums for e in one.due(24)])
        wo = wout_rows(wout_s, wout_o)
        gg = jnp.zeros((1, d), f32)
        gs = gg
        gbb = gg
        stores = []
        for t in range(tokens // C):
            rows = pl.ds(t * C, C)
            mid = middle[rows, :]
            ct = cotv[rows, :]
            acc[rows, :] = mid + acc[rows, :] + back_bias[...]
            n, rsq = stats(mid)
            e = gacc[rows, :]
            gg = gg + jnp.sum(e * n, 0, keepdims=True)
            gs = gs + jnp.sum(e, 0, keepdims=True)
            gbb = gbb + jnp.sum(ct, 0, keepdims=True)
            eg = e * gain[...]
            gm = ct + rsq * (eg - jnp.mean(eg, -1, keepdims=True) - n * jnp.mean(eg * n, -1, keepdims=True))
            gacc[rows, :] = gm
            g = split(gm)
            n2h[rows, :], n2l[rows, :] = g
            coth[rows, :], cotl[rows, :] = split(mixv[rows, :])
            mixv[rows, :] = dot3(g, wo, NT)
            for k, (src, dst) in enumerate(((acc, out), (gacc, gmid), (mixv, gmix))):
                stores.append(pltpu.make_async_copy(src.at[t * C : (t + 1) * C], dst.at[t * C : (t + 1) * C], load.at[k, t]))
                stores[-1].start()
        go = dot3((coth[...], cotl[...]), (n2h[...], n2l[...]), TN)
        for slot in range(go.shape[0] // 128):
            flat_put(gout.at[slot % 2], slot // 2 * d // 8, go[slot * 128 : (slot + 1) * 128])
        for parity in range(2):
            smalls[parity, 0:2] = jnp.zeros((2, d), f32)
            smalls[parity, 2:3] = gg
            smalls[parity, 3:4] = gs
            smalls[parity, 4:5] = gbb
            used = groups * BH // d
            for r in range(used):
                per = d // BH
                smalls[parity, 5 + r : 6 + r] = jnp.concatenate(
                    [gbin[2 * (r * per + c) + parity : 2 * (r * per + c) + parity + 1] for c in range(per)], 1
                )
            if used < 3:
                smalls[parity, 5 + used :] = jnp.zeros((3 - used, d), f32)
        last = unpack(done.at[0], 0, (BH, d), gback0, store.at[0:6]) + unpack(
            done.at[0], d * BH // 1024, (d, BH), gin0, store.at[6:12]
        )
        for copy in last:
            copy.start()
        run([e for one in sums for e in one.due(25)])
        for g in range(1, groups):
            left = done if sums[g].last >= bits else both.at[1]
            last.append(pltpu.make_async_copy(left.at[g], sums_left.at[g - 1], store.at[11 + g]))
            last[-1].start()
        for copy in stores + last:
            copy.wait()


POLLS = 4
BWD_POLLS = (
    [0, 0, 0, 0, 0, 0, 0, 3, 5],
    [0, 0, 0, 0, 0, 3, 5, 7, 9],
    [0, 0, 3, 5, 7, 9, 11, 13, 15],
    [3, 5, 7, 9, 11, 13, 15, 16, 16],
    [8, 11, 13, 15, 16, 16, 16, 16, 16],
    None,
)


def small_stages(bits):
    return [(shift, min(2, bits - shift)) for shift in range(0, bits, 2)]


def attn_bwd(
    bits,
    gain, shift, segs, fback, gm, mixed, invt, sq, sk, vv, qfh, qfl, kfh, kfl, ah, al, sp, small,
    x, gmid, w_hi, w_lo, sums_left, gout,
    ginputs, gback1, gin1, gout_out, qkv0, qkv1, smalls,
    n1h, n1l, xv, gv, wh, wl, gh, gl, masks, segc, segr,
    done, ffn, ffn_in, heads, heads_send, heads_mp, heads_in, heads_done, outs, outs_send, outs_mp, outs_in, outs_done,
    sm, sm_in,
    load, store, ss, rs, mp_ss, mp_rs, sm_ss, sm_rs,
):
    slot = pl.program_id(0)
    slots = pl.num_programs(0)
    tokens, d = x.shape
    chunks = tokens // C
    scale = 64.0 ** -0.25
    dp = lax.axis_index("dp")
    other = {"mp": 1 - lax.axis_index("mp")}
    gtiles = gout.shape[1]
    qtiles = d // 8
    left = sums_left.shape[0]
    stages = small_stages(bits)
    polled = [
        Sum(ffn if FFN_LAST[j + 1] * 2 * bits // 8 < bits else None, ffn_in, done.at[j], ss.at[j], rs.at[j], dp, bits,
            BWD_POLLS[j], FFN_LAST[j + 1])
        for j in range(left)
    ]
    outs_sum = Sum(outs, outs_in, outs_done, ss.at[left], rs.at[left], dp, bits, BWD_POLLS[left])
    half_sum, tail_sum = (
        Sum(heads.at[j], heads_in.at[j], heads_done.at[j], ss.at[left + 1 + j], rs.at[left + 1 + j], dp, bits, BWD_POLLS[left + 1 + j])
        for j in range(2)
    )
    polled += [outs_sum, half_sum]

    def to_sibling(src, dst, i):
        return pltpu.make_async_remote_copy(
            src_ref=src, dst_ref=dst, send_sem=mp_ss.at[i], recv_sem=mp_rs.at[i], device_id=other, device_id_type=MESH
        )

    swap_out = to_sibling(outs_send, outs_mp, 0)
    swap_heads = [to_sibling(heads_send.at[j], heads_mp.at[j], 1 + j) for j in range(2)]
    loads = [
        pltpu.make_async_copy(*pair, load.at[i])
        for i, pair in enumerate((
            (x, xv), (gout.at[0], outs_send), (gout.at[1], outs.at[0:gtiles]),
            (w_hi, wh), (w_lo, wl), (gmid, gv),
        ))
    ]
    resumes = [
        pltpu.make_async_copy(sums_left.at[j], done.at[j] if polled[j].total is None else ffn, load.at[6 + j])
        for j in range(left)
    ]

    def run(todo):
        for one, p, k in todo:
            if one is outs_sum and k == 0 and p is one.parts[0]:
                swap_out.wait()
                outs[0:gtiles] = outs[0:gtiles] + outs_mp[...]
            one.event(p, k)

    def due(q):
        return [e for one in polled for e in one.due(q)]

    def poll(q_in_slot):
        for step in range(4):
            todo = due(step * POLLS + q_in_slot)
            if todo:

                @pl.when(slot == step)
                def _():
                    run(todo)

    @pl.when(slot == 0)
    def _():
        for copy in resumes + loads:
            copy.start()
        for copy in resumes:
            copy.wait()
        greet(dp, sorted({1 << b for b in range(bits)} | {j << s for s, w in stages for j in range(1, 1 << w)}), other)
        make_masks(masks, segc, segr, segs)
        for r, used in ((outs, gtiles), (heads.at[0], 3 * qtiles), (heads.at[1], 3 * qtiles)):
            if used < r.shape[0]:
                r[used:] = jnp.zeros((r.shape[0] - used, 8, 128), f32)
        for copy in loads[:3]:
            copy.wait()
        swap_out.start()

    @pl.when(slot == 0)
    def _():
        for c in range(chunks):
            rows = pl.ds(c * C, C)
            n, _ = stats(xv[rows, :])
            n1h[:, rows], n1l[:, rows] = split((n * gain[...] + shift[...]).T)

    lane = lanes(C)
    at = pl.ds(pl.multiple_of(slot * 128, 128), 128)
    keys_one = jnp.where((lane == 64) | (lane == 66), 1.0, 0.0)

    def put(which, rows, g):
        gh[which, rows, at], gl[which, rows, at] = split(g)

    def back(which, rows, grads, feats, s):
        total = None
        sums = []
        for h in range(2):
            dd = grads[h] * (feats[h][0].astype(f32) + feats[h][1].astype(f32))
            sums.append(jnp.sum(dd, -1, keepdims=True))
            for half in split(dd):
                term = dot(half, fback[h], NT)
                total = term if total is None else total + term
        put(which, rows, (fold(total) - s * jnp.where(lane < 64, sums[0], sums[1])) * scale)

    grad = [None, None]
    for c in reversed(range(chunks)):
        poll(chunks - 1 - c)
        rows = pl.ds(c * C, C)
        cont, tailk, carry = seg_flags(segc, segr, c)
        u = gm[rows, :] * invt[rows, :]
        prod = u * mixed[rows, :]
        weights = [-jnp.sum(jnp.where(lane // 64 == h, prod, 0.0), -1, keepdims=True) for h in range(2)]
        ut = u.T
        wt = jnp.where(lane < 64, weights[0], weights[1]).T
        ru = right_pack(u, weights, lane)
        lv = left_pack(vv[rows, :], keys_one, lane)
        gq, gk, gvt, qfs, kfs = [], [], [], [], []
        for h in range(2):
            qf = (qfh[h, rows, :], qfl[h, rows, :])
            kf = (kfh[h, rows, :], kfl[h, rows, :])
            ga = split(dot(ru[h], lv[h], NT) * masks[c])
            gqf = dot3(ga, kf)
            gkf = dot3(ga, qf, TN)
            uth = ut[h * 64 : (h + 1) * 64]
            gvh = dot3(split(uth), (ah[h, rows, :], al[h, rows, :]))
            if c > 0:
                gqf = gqf + cont[0] * dot(ru[h], sp[h, c - 1])
            if c < chunks - 1:
                gkf = gkf + tailk[0] * dot(lv[h], stack_rows(grad[h], (0, 0, 1)))
                gvh = gvh + tailk[1] * dot3(split(grad[h][:64]), kf, NT)
            if c > 0:
                fresh = dot3(split(with_row(uth, wt[h * 64 : h * 64 + 1], 0) * cont[1]), qf)
                grad[h] = fresh if c == chunks - 1 else fresh + carry * grad[h]
            gq.append(gqf)
            gk.append(gkf)
            gvt.append(gvh)
            qfs.append(qf)
            kfs.append(kf)
        back(0, rows, gq, qfs, sq[rows, :])
        back(1, rows, gk, kfs, sk[rows, :])
        put(2, rows, jnp.concatenate(gvt, 0).T)

    def weight_grads(flat):
        g = dot3(
            (n1h[...], n1l[...]), [jnp.concatenate([r[i, :, at] for i in range(3)], 1) for r in (gh, gl)]
        )
        flat_put(flat, 0, g)

    for j in range(2):

        @pl.when(slot == 2 * j)
        def _():
            weight_grads(heads_send.at[j])
            swap_heads[j].start()

    def own_grads(j):
        weight_grads(heads.at[j])
        swap_heads[j].wait()
        used = 3 * qtiles
        heads[j, 0:used] = heads[j, 0:used] + heads_mp[j]

    @pl.when(slot == 1)
    def _():
        own_grads(0)

    @pl.when(slot == slots - 1)
    def _():
        own_grads(1)
        run([(tail_sum, p, 0) for p in tail_sum.parts])
        for copy in loads[3:]:
            copy.wait()
        run([e for one in polled[:left] for e in one.due(16)])
        waiting = [[[e for e in one.due(16) if e[2] == k] for k in range(2 * bits + 1)] for one in polled[left:]]
        waiting = [[e for e in chain if e] for chain in waiting]
        following = [[(tail_sum, p, k) for p in tail_sum.parts] for k in range(1, 2 * bits + 1)]

        def half_next():
            for chain in waiting:
                if chain:
                    run(chain.pop(0))

        def tail_next():
            if following:
                run(following.pop(0))

        stores = []
        for g in range(left):
            stores += unpack(done.at[g], 0, (BH, d), gback1.at[g * BH : (g + 1) * BH], store.at[12 * g : 12 * g + 6])
            stores += unpack(
                done.at[g], d * BH // 1024, (d, BH), gin1.at[:, g * BH : (g + 1) * BH], store.at[12 * g + 6 : 12 * g + 12]
            )
        for copy in stores:
            copy.start()
        half_next()
        gg = jnp.zeros((1, d), f32)
        gs = gg
        for c in range(chunks):
            rows = pl.ds(c * C, C)
            n, rsq = stats(xv[rows, :])
            e = jnp.zeros((C, d), f32)
            for i in range(3):
                e = e + dot3((gh[i, rows, :], gl[i, rows, :]), (wh[i], wl[i]), NT)
            gg = gg + jnp.sum(e * n, 0, keepdims=True)
            gs = gs + jnp.sum(e, 0, keepdims=True)
            eg = e * gain[...]
            gv[rows, :] = gv[rows, :] + rsq * (
                eg - jnp.mean(eg, -1, keepdims=True) - n * jnp.mean(eg * n, -1, keepdims=True)
            )
            tail_next()
            half_next()
        rows_store = [pltpu.make_async_copy(gv, ginputs, store.at[12 * left])]
        rows_store[0].start()
        sm[0] = jnp.concatenate([gg, gs, small[0, 2:]], 0)
        first = to_sibling(sm.at[0], sm_in.at[0], 3)
        first.start()
        tail_next()
        while any(waiting):
            half_next()
        base = 12 * left + 1
        for s in range(gtiles * 8 // d):
            rows_store += unpack(
                outs_done, s * d // 8, (128, d), gout_out.at[s * 128 : (s + 1) * 128], store.at[base + 4 * s : base + 4 * s + 4]
            )
        base += gtiles * 32 // d
        for c in range(3):
            rows_store += unpack(heads_done.at[0], c * qtiles, (d, 128), qkv0.at[c], store.at[base + c : base + c + 1])
        for copy in rows_store[1:]:
            copy.start()
        first.wait()
        sm[1] = jnp.concatenate([gg, gs, small[1, 2:]], 0) + sm_in[0]
        for i, (shift, width) in enumerate(stages):
            digit = (dp >> shift) & ((1 << width) - 1)
            sends = [
                pltpu.make_async_remote_copy(
                    src_ref=sm.at[i + 1], dst_ref=sm_in.at[1 + 4 * i + digit], send_sem=sm_ss.at[3 * i + j - 1],
                    recv_sem=sm_rs.at[3 * i + j - 1], device_id={"dp": dp ^ (j << shift)}, device_id_type=MESH,
                )
                for j in range(1, 1 << width)
            ]
            for copy in sends:
                copy.start()
            sm_in[1 + 4 * i + digit] = sm[i + 1]
            tail_next()
            for copy in sends:
                copy.wait()
            total = sm_in[1 + 4 * i]
            for j in range(1, 1 << width):
                total = total + sm_in[1 + 4 * i + j]
            sm[i + 2] = total
        while following:
            tail_next()
        smalls[...] = sm[len(stages) + 1]
        ends = []
        base += 3
        for c in range(3):
            ends += unpack(heads_done.at[1], c * qtiles, (d, 128), qkv1.at[c], store.at[base + c : base + c + 1])
        for copy in ends:
            copy.start()
        for copy in stores + rows_store + ends:
            copy.wait()


def whole(shape):
    return pl.BlockSpec(shape, lambda i: (0,) * len(shape))


def params(**more):
    return pltpu.CompilerParams(vmem_limit_bytes=VMEM_LIMIT, dimension_semantics=("arbitrary",), **more)


def sds(shape, dtype=f32):
    return jax.ShapeDtypeStruct(shape, dtype)


ANY = pl.BlockSpec(memory_space=pl.ANY)


def run_attn_fwd(x, gain, shift, segs, w, features):
    t, d = x.shape
    heads, _, m = features.shape
    cols = w.shape[2]
    chunks = t // C
    slot = lambda i: (i % 2) * 2 + 1 - i // 2
    per_pair = pl.BlockSpec((t, 128), lambda i: (0, slot(i)))
    per_head = pl.BlockSpec((2, t, m), lambda i: (slot(i), 0, 0))
    sem = lambda *n: pltpu.SemaphoreType.DMA(n)
    return pl.pallas_call(
        attn_fwd,
        grid=(heads,),
        in_specs=[whole((t, d)), whole((1, d)), whole((1, d)), whole(segs.shape), ANY, ANY],
        out_specs=[per_pair] * 3 + [per_head] * 4 + [pl.BlockSpec((2, t, C), lambda i: (slot(i), 0, 0))] * 2
        + [pl.BlockSpec((2, chunks - 1, 256, m), lambda i: (slot(i), 0, 0, 0))] + [per_pair] * 2
        + [pl.BlockSpec((2, 256, m), lambda i: (slot(i), 0, 0))] + [pl.BlockSpec((3, d, 128), lambda i: (0, 0, slot(i)))] * 2,
        out_shape=[sds((t, 2 * cols))] * 3 + [sds((2 * heads, t, m), bf16)] * 4 + [sds((2 * heads, t, C), bf16)] * 2
        + [sds((2 * heads, chunks - 1, 256, m), bf16)] + [sds((t, 2 * cols))] * 2 + [sds((2 * heads, 256, m), bf16)]
        + [sds((3, d, 2 * cols), bf16)] * 2,
        scratch_shapes=[pltpu.VMEM((t, cols), f32)] * 3 + [pltpu.VMEM((t, d), bf16)] * 2 + [pltpu.VMEM((chunks, C, C), f32)]
        + [pltpu.VMEM((t, 128), f32), pltpu.VMEM((1, t), f32)] + [pltpu.VMEM((2,) + w.shape, f32), pltpu.VMEM((2,) + features.shape, f32), sem(2), sem(2), sem(2)],
        cost_estimate=pl.CostEstimate(flops=60 * t * d * d, bytes_accessed=80 * t * d * 4, transcendentals=2 * t * d),
        compiler_params=params(collective_id=3, has_side_effects=True),
        name="attn_fwd",
    )(x, gain, shift, segs, w, features)


def run_ffn(x, mixed, wout_s, wout_o, gain, shift, back_bias, cot, w_s, w_o, dp_size):
    t, d = x.shape
    hid = w_s[0].shape[1]
    cols = mixed.shape[1]
    bits = dp_size.bit_length() - 1
    groups = hid // BH
    tiles = 2 * d * BH // 1024
    weights = [
        pl.BlockSpec((d, BH), lambda i: (0, i // 2)), pl.BlockSpec((1, BH), lambda i: (0, i // 2)),
        pl.BlockSpec((BH, d), lambda i: (i // 2, 0)),
    ]
    half = (2, cols // 2 * d // 1024, 8, 128)
    sem = lambda *n: pltpu.SemaphoreType.DMA(n)
    vm = lambda shape, dtype=f32: pltpu.VMEM(shape, dtype)
    block = (groups, tiles, 8, 128)
    return pl.pallas_call(
        functools.partial(ffn, bits),
        grid=(2 * groups,),
        in_specs=[whole(wout_s.shape), whole(wout_o.shape)] + [whole((1, d))] * 3 + weights * 2 + [ANY] * 3,
        out_specs=[ANY] * 3 + [whole(half), whole((2, 8, d))] + [ANY] * 3,
        out_shape=[sds((t, d)), sds((t, d)), sds((t, cols)), sds(half), sds((2, 8, d)),
                   sds((BH, d)), sds((d, BH)), sds((groups - 1,) + block[1:])],
        scratch_shapes=[vm((t, cols)), vm((t, d)), vm((t, d)), vm((t, d)), vm((t, d))] + [vm((t, d), bf16)] * 4
        + [vm((t, BH), bf16)] * 4
        + [vm((2,) + block), vm(block)] + [vm(block)] * 2 + [vm((2 * groups, BH))]
        + [sem(3, t // C), sem(11 + groups), sem(groups), sem(groups), sem(groups, 3, 2 * bits), sem(groups, 3, 2 * bits)],
        compiler_params=params(collective_id=1, has_side_effects=True),
        name="ffn",
    )(wout_s, wout_o, gain, shift, back_bias, *w_s, *w_o, x, mixed, cot)


def run_attn_bwd(x, gain, shift, segs, gm, saved, small, gmid, sums_left, gout, dp_size):
    sq, sk, vv, qfh, qfl, kfh, kfl, ah, al, sp, mixed, invt, fback, wh, wl = saved
    t, d = x.shape
    heads, _, m = fback.shape
    cols = gm.shape[1]
    chunks = t // C
    bits = dp_size.bit_length() - 1
    up = lambda n: -(-n // dp_size) * dp_size
    stages = len(small_stages(bits))
    tiles = lambda n: pltpu.VMEM((n, 8, 128), f32)
    left, nf = sums_left.shape[:2]
    ng, nq = gout.shape[1], 3 * d // 8
    pair = lambda n: pltpu.VMEM((2, n, 8, 128), f32)
    sem = lambda *n: pltpu.SemaphoreType.DMA(n)
    per_slot = pl.BlockSpec((t, 128), lambda p: (0, p))
    per_head = pl.BlockSpec((2, t, m), lambda p: (p, 0, 0))
    rows = small.shape[1]
    return pl.pallas_call(
        functools.partial(attn_bwd, bits),
        grid=(heads // 2,),
        in_specs=[
            whole((1, d)), whole((1, d)), whole(segs.shape), pl.BlockSpec((2, 256, m), lambda p: (p, 0, 0)),
        ] + [per_slot] * 6 + [per_head] * 4 + [pl.BlockSpec((2, t, C), lambda p: (p, 0, 0))] * 2
        + [pl.BlockSpec((2, chunks - 1, 256, m), lambda p: (p, 0, 0, 0))] + [whole(small.shape)] + [ANY] * 6,
        out_specs=[ANY] * 6 + [whole((rows, d))],
        out_shape=[sds((t, d)), sds((left * BH, d)), sds((d, left * BH)), sds((cols // 2, d)), sds((3, d, 128)), sds((3, d, 128)),
                   sds((rows, d))],
        scratch_shapes=[pltpu.VMEM((d, t), bf16)] * 2 + [pltpu.VMEM((t, d), f32)] * 2 + [pltpu.VMEM((3, d, cols), bf16)] * 2
        + [pltpu.VMEM((3, t, cols), bf16)] * 2 + [pltpu.VMEM((chunks, C, C), f32), pltpu.VMEM((t, 128), f32), pltpu.VMEM((1, t), f32)]
        + [pltpu.VMEM((left, nf, 8, 128), f32), tiles(nf), tiles(nf)] + [pair(up(nq)), pair(nq), pair(nq), pair(up(nq)), pair(up(nq))]
        + [tiles(up(ng)), tiles(ng), tiles(ng), tiles(up(ng)), tiles(up(ng))]
        + [pltpu.VMEM((stages + 2, rows, d), f32), pltpu.VMEM((4 * stages + 1, rows, d), f32)]
        + [sem(6 + left), sem(12 * left + 1 + ng * 32 // d + 6), sem(left + 3, 3, 2 * bits), sem(left + 3, 3, 2 * bits), sem(4), sem(4), sem(3 * stages), sem(3 * stages)],
        compiler_params=params(collective_id=2, has_side_effects=True),
        name="attn_bwd",
    )(gain, shift, segs, fback, gm, mixed, invt, sq, sk, vv, qfh, qfl, kfh, kfl, ah, al, sp, small,
      x, gmid, wh, wl, sums_left, gout)


def place(output, ginputs, gback0, gback1, gin0, gin1, gout, qkv0, qkv1, small, o1, o2, o3, o4, o5, o6, obias, *vectors):
    used = obias.shape[0] // small.shape[1]
    for r in range(used):
        obias[r * small.shape[1] : (r + 1) * small.shape[1]] = small[5 + r]
    for r, vector in enumerate(vectors):
        vector[...] = small[r]
    o1[...] = output[...]
    o2[...] = ginputs[...]
    o4[:, : gin0.shape[1]] = gin0[...]
    o4[:, gin0.shape[1] :] = gin1[...]
    o5[...] = gout[...]
    o6[:, :, :128] = qkv0[...]
    o6[:, :, 128:] = qkv1[...]
    first = pl.program_id(0) * o3.shape[0] < BH

    @pl.when(first)
    def _():
        o3[...] = gback0[...]

    @pl.when(jnp.logical_not(first))
    def _():
        o3[...] = gback1[...]


def run_place(output, ginputs, gback0, gback1, gin0, gin1, gout, qkv0, qkv1, small):
    steps = 4
    back = (gback0.shape[0] + gback1.shape[0], gback0.shape[1])
    ins = (gin0.shape[0], gin0.shape[1] + gin1.shape[1])
    qkv = qkv0.shape[:2] + (2 * qkv0.shape[2],)
    rows = lambda shape: pl.BlockSpec((shape[0] // steps, shape[1]), lambda i: (i, 0))
    mids = lambda shape: pl.BlockSpec((shape[0], shape[1] // steps, shape[2]), lambda i: (0, i, 0))
    size = back[0] // steps
    n0 = gback0.shape[0] // size
    return pl.pallas_call(
        place,
        grid=(steps,),
        in_specs=[
            rows(output.shape), rows(ginputs.shape),
            pl.BlockSpec((size, back[1]), lambda i: (jnp.minimum(i, n0 - 1), 0)),
            pl.BlockSpec((size, back[1]), lambda i: (jnp.maximum(i - n0, 0), 0)),
            rows(gin0.shape), rows(gin1.shape), rows(gout.shape), mids(qkv0.shape), mids(qkv1.shape), whole(small.shape),
        ],
        out_specs=[rows(output.shape), rows(ginputs.shape), rows(back), rows(ins), rows(gout.shape), mids(qkv), whole(back[:1])] + [whole(back[1:])] * 5,
        out_shape=[sds(output.shape), sds(ginputs.shape), sds(back), sds(ins), sds(gout.shape), sds(qkv), sds(back[:1])] + [sds(back[1:])] * 5,
        compiler_params=params(),
        name="place",
    )(output, ginputs, gback0, gback1, gin0, gin1, gout, qkv0, qkv1, small)


def body(
    dp_size,
    inputs, segment_ids, first_gain, first_shift, qkv_weight, out_weight, features,
    second_gain, second_shift, in_weight, in_bias, back_weight, back_bias, cotangent,
):
    swap = [(0, 1), (1, 0)]

    def other(array):
        return lax.ppermute(array, "mp", swap)

    row = lambda v: v.reshape(1, -1)
    out_s = other(out_weight)
    in_s, bin_s, back_s = other(in_weight), other(in_bias), other(back_weight)
    g1, s1, g2, s2 = row(first_gain), row(first_shift), row(second_gain), row(second_shift)
    saved = run_attn_fwd(inputs, g1, s1, segment_ids, qkv_weight, features.swapaxes(1, 2))
    output, gmid, gmix, gout, small, gback0, gin0, sums_left = run_ffn(
        inputs, saved[10], out_s, out_weight, g2, s2, row(back_bias), cotangent,
        (in_s, row(bin_s), back_s), (in_weight, row(in_bias), back_weight), dp_size,
    )
    g_inputs, gback1, gin1, g_out, qkv0, qkv1, small = run_attn_bwd(
        inputs, g1, s1, segment_ids, gmix, saved, small, gmid, sums_left, gout, dp_size,
    )
    output, g_inputs, gback, gin, g_out, gqkv, gbin, *small = run_place(
        output, g_inputs, gback0, gback1, gin0, gin1, g_out, qkv0, qkv1, small
    )
    return (output, g_inputs, small[0], small[1], gqkv, g_out, small[2], small[3], gin, gbin, gback, small[4])


def solution(mesh):
    rows = P(("dp", "mp"), None)
    return jax.shard_map(
        functools.partial(body, mesh.shape["dp"]),
        mesh=mesh,
        in_specs=(
            rows, P("dp", None), P(), P(), P(None, None, "mp"), P("mp", None), P("mp", None, None),
            P(), P(), P(None, "mp"), P("mp"), P("mp", None), P(), rows,
        ),
        out_specs=(
            rows, rows, P(), P(), P(None, None, "mp"), P("mp", None), P(), P(), P(None, "mp"), P("mp"), P("mp", None), P(),
        ),
        check_vma=False,
    )
```

```python
import functools
import math

import jax
import jax.numpy as jnp
from jax import lax
from jax.experimental import pallas as pl
from jax.experimental.pallas import tpu as pltpu
from jax.sharding import PartitionSpec as P

f32 = jnp.float32
bf16 = jnp.bfloat16
EPS = 1e-05
C = 256
BH = 256
VMEM_LIMIT = 60 * 1024 * 1024
MESH = pl.DeviceIdType.MESH
NN = (((1,), (0,)), ((), ()))
NT = (((1,), (1,)), ((), ()))
TN = (((0,), (0,)), ((), ()))


def split(x):
    hi = x.astype(bf16)
    return hi, (x - hi.astype(f32)).astype(bf16)


def dot(a, b, dims=NN):
    return lax.dot_general(a, b, dims, preferred_element_type=f32)


def dot3(a, b, dims=NN):
    left, right = dims[0][0][0], dims[0][1][0]
    return dot(jnp.concatenate([a[0], a[0], a[1]], left), jnp.concatenate([b[0], b[1], b[0]], right), dims)


def stats(v):
    mean = jnp.mean(v, -1, keepdims=True)
    centred = v - mean
    rs = lax.rsqrt(jnp.mean(centred * centred, -1, keepdims=True) + EPS)
    return centred * rs, rs


def lanes(n):
    return lax.broadcasted_iota(jnp.int32, (n, 128), 1)


def half_split(x):
    hi = x.astype(bf16).astype(f32)
    return hi, x - hi


def swap_halves(x):
    return pltpu.roll(x, 64, 1)


def pack(first, second):
    return jnp.concatenate([first.astype(bf16), second.astype(bf16)], 1)


def left_pack(x, extra, lane):
    hi, lo = half_split(x)
    hi_turned = swap_halves(hi)
    return (
        pack(jnp.where(lane < 64, hi, swap_halves(lo)), jnp.where(lane < 64, hi, extra)),
        pack(jnp.where(lane < 64, hi_turned, lo), jnp.where(lane < 64, hi_turned, extra)),
    )


def right_pack(x, extras, lane):
    hi, lo = half_split(x)
    hi_turned = swap_halves(hi)

    def second(low, e):
        e_hi, e_lo = half_split(e)
        return jnp.where(lane < 64, low, jnp.where(lane < 66, e_hi, jnp.where(lane == 66, e_lo, 0.0)))

    return (
        pack(jnp.where(lane < 64, hi, hi_turned), second(lo, extras[0])),
        pack(jnp.where(lane < 64, hi_turned, hi), second(swap_halves(lo), extras[1])),
    )


def stack_rows(x, order):
    halves = half_split(x)
    row = lax.broadcasted_iota(jnp.int32, (16, x.shape[1]), 0)
    last = jnp.zeros((16, x.shape[1]), f32)
    for i, which in enumerate(order):
        last = jnp.where(row == i, halves[which][64:65], last)
    blocks = [halves[which][:64] for which in order] + [last, jnp.zeros((48, x.shape[1]), f32)]
    return jnp.concatenate(blocks, 0).astype(bf16)


def wide(x):
    hi, lo = split(x)
    return jnp.concatenate([hi, lo], 1)


def fold(x):
    return x[:, :128] + x[:, 128:]


def with_row(x, row, at):
    place = lax.broadcasted_iota(jnp.int32, (16, x.shape[1]), 0)
    return jnp.concatenate([x, jnp.where(place == at, row, 0.0)], 0)


def make_masks(masks, segc, segr, segs):
    ids = segs[pl.ds(lax.axis_index("mp"), 1), :].astype(f32)
    segr[...] = ids
    for c in range(segc.shape[0] // C):
        segc[c * C : (c + 1) * C, :] = jnp.broadcast_to(ids[:, c * C : (c + 1) * C], (128, C)).T
    row = lax.broadcasted_iota(jnp.int32, (C, C), 0)
    col = lax.broadcasted_iota(jnp.int32, (C, C), 1)
    for c in range(segc.shape[0] // C):
        same = segc[c * C : (c + 1) * C, 0:1] == segr[:, c * C : (c + 1) * C]
        masks[c] = jnp.where(same & (row >= col), 1.0, 0.0)


def seg_flags(segc, segr, c):
    rows, row = segc[c * C : (c + 1) * C, 0:1], segr[:, c * C : (c + 1) * C]
    last = segc[(c + 1) * C - 1 : (c + 1) * C, 0:1]
    tail = ((rows == last).astype(f32), (row == last).astype(f32))
    if c == 0:
        return None, tail, None
    before = segc[c * C - 1 : c * C, 0:1]
    return ((rows == before).astype(f32), (row == before).astype(f32)), tail, (last == before).astype(f32)


def attn_fwd(
    x, gain, shift, segs, w, features,
    sq, sk, vv, qfh, qfl, kfh, kfl, ah, al, sp, mixed, invt, fback, wh, wl,
    qs, ks, vs, n1h, n1l, masks, segc, segr, wv, fv, load, mp_ss, mp_rs,
):
    step = pl.program_id(0)
    side = step // 2
    pair = step % 2
    tokens = x.shape[0]
    chunks = tokens // C
    scale = 64.0 ** -0.25
    other = {"mp": 1 - lax.axis_index("mp")}
    swaps = [
        pltpu.make_async_remote_copy(
            src_ref=ref.at[0], dst_ref=ref.at[1], send_sem=mp_ss.at[i], recv_sem=mp_rs.at[i], device_id=other, device_id_type=MESH
        )
        for i, ref in enumerate((wv, fv))
    ]

    def project(which):
        ws = [split(wv[which, i]) for i in range(3)]
        for c in range(chunks):
            rows = pl.ds(c * C, C)
            n1 = (n1h[rows, :], n1l[rows, :])
            qs[rows, :] = dot3(n1, ws[0]) * scale
            ks[rows, :] = dot3(n1, ws[1]) * scale
            vs[rows, :] = dot3(n1, ws[2])

    @pl.when(step == 0)
    def _():
        own = [pltpu.make_async_copy(src, dst.at[0], load.at[i]) for i, (src, dst) in enumerate(((w, wv), (features, fv)))]
        for copy in own:
            copy.start()
        barrier = pltpu.get_barrier_semaphore()
        pl.semaphore_signal(barrier, inc=1, device_id=other, device_id_type=MESH)
        for c in range(chunks):
            rows = pl.ds(c * C, C)
            n, _ = stats(x[rows, :])
            n1h[rows, :], n1l[rows, :] = split(n * gain[...] + shift[...])
        make_masks(masks, segc, segr, segs)
        for copy in own:
            copy.wait()
        pl.semaphore_wait(barrier, 1)
        for copy in swaps:
            copy.start()
        project(0)

    @pl.when(step == 2)
    def _():
        for copy in swaps:
            copy.wait()
        project(1)

    at = pl.ds(pl.multiple_of(pair * 128, 128), 128)
    for i in range(3):
        wh[i], wl[i] = split(wv[side, i, :, at])
    lane = lanes(C)
    m = features.shape[2]
    ones = jnp.where(lane == 64, 1.0, 0.0)
    fright = []
    for h in range(2):
        fhi, flo = half_split(fv[side, pair * 2 + h])
        gap = jnp.zeros_like(fhi)
        fright.append(jnp.concatenate([fhi, fhi, flo, gap], 0).astype(bf16))
        fback[h] = jnp.concatenate([gap, fhi, gap, flo] if h else [fhi, gap, flo, gap], 0).astype(bf16)

    def feats(s):
        squares = s * s
        left = left_pack(s, 0.0, lane)
        out = []
        for h in range(2):
            half = 0.5 * jnp.sum(jnp.where(lane // 64 == h, squares, 0.0), -1, keepdims=True) + 0.5 * math.log(m)
            out.append(split(jnp.exp(dot(left[h], fright[h]) - half)))
        return out

    state = [None, None]
    for c in range(chunks):
        rows = pl.ds(c * C, C)
        q, k, v = qs[rows, at], ks[rows, at], vs[rows, at]
        sq[rows, :] = q
        sk[rows, :] = k
        vv[rows, :] = v
        qf = feats(q)
        kf = feats(k)
        cont, tail, carry = seg_flags(segc, segr, c)
        vt = v.T
        nums = []
        for h in range(2):
            qfh[h, rows, :], qfl[h, rows, :] = qf[h]
            kfh[h, rows, :], kfl[h, rows, :] = kf[h]
            va = wide(jnp.where(lane < 64, swap_halves(v) if h else v, ones))
            a = split(dot3(qf[h], kf[h], NT) * masks[c])
            ah[h, rows, :], al[h, rows, :] = a
            num = fold(dot(a[0], va)) + dot(a[1], va[:, :128])
            if c > 0:
                hi, lo = split(state[h])
                gap = jnp.zeros((48, m), bf16)
                both = jnp.concatenate([hi, gap, lo, gap], 0)
                num = num + cont[0] * (fold(dot(qf[h][0], both, NT)) + dot(qf[h][1], both[:128], NT))
            if c < chunks - 1:
                vat = with_row(vt[h * 64 : (h + 1) * 64], 1.0, 0)
                fresh = dot3(split(vat * tail[1]), kf[h])
                state[h] = fresh if c == 0 else fresh + carry * state[h]
                sp[h, c] = stack_rows(state[h], (0, 1, 0))
            nums.append(num)
        inv = [1.0 / num[:, 64:65] for num in nums]
        mixed[rows, :] = jnp.where(lane < 64, nums[0] * inv[0], swap_halves(nums[1] * inv[1]))
        invt[rows, :] = jnp.where(lane < 64, inv[0], inv[1])


def flat_put(flat, start, value):
    tiles = value.shape[0] // 8
    for j in range(value.shape[1] // 128):
        flat[start + j * tiles : start + (j + 1) * tiles] = value[:, j * 128 : (j + 1) * 128].reshape(tiles, 8, 128)


def wout_rows(wout_s, wout_o):
    s, o = wout_s[...], wout_o[...]
    parts = [w[i : i + 128] for i in range(0, s.shape[0], 128) for w in (s, o)]
    return split(jnp.concatenate(parts, 0))


class Sum:
    def __init__(self, total, landed, done, send, recv, me, bits, polls, first=0, last=8):
        self.total, self.landed, self.done = total, landed, done
        self.send, self.recv, self.me, self.bits, self.polls = send, recv, me, bits, polls
        self.first, self.last = first * 2 * bits // 8, last * 2 * bits // 8
        units = done.shape[0] >> bits
        cuts = (0, units * 6 // 16, units * 12 // 16, units)
        self.parts = []
        base = 0
        for i in range(3):
            n = (cuts[i + 1] - cuts[i]) << bits
            if n:
                turn = [0, (bits + 1) // 4, (bits + 1) * 2 // 4][i]
                low = list(range(bits - 1))
                self.parts.append((base, n, low[turn:] + low[:turn] + [bits - 1], i))
            base += n

    def offset(self, part, step):
        base, n, order, _ = part
        for k in range(step):
            base = base + ((self.me >> order[k]) & 1) * (n >> (k + 1))
        return base

    def halving(self, part, step):
        base, n, order, i = part
        half = n >> (step + 1)
        mine = (self.me >> order[step]) & 1
        return pltpu.make_async_remote_copy(
            src_ref=self.total.at[pl.ds(self.offset(part, step) + (1 - mine) * half, half)],
            dst_ref=self.landed.at[pl.ds(base + n - (n >> step), half)],
            send_sem=self.send.at[i, step],
            recv_sem=self.recv.at[i, step],
            device_id={"dp": self.me ^ (1 << order[step])},
            device_id_type=MESH,
        )

    def add(self, part, step):
        base, n, order, _ = part
        half = n >> (step + 1)
        mine = (self.me >> order[step]) & 1
        keep = pl.ds(self.offset(part, step) + mine * half, half)
        to = self.done if step == self.bits - 1 else self.total
        to[keep] = self.total[keep] + self.landed[pl.ds(base + n - (n >> step), half)]

    def doubling(self, part, step):
        _, n, order, i = part
        at = pl.ds(self.offset(part, step + 1), n >> (step + 1))
        return pltpu.make_async_remote_copy(
            src_ref=self.done.at[at],
            dst_ref=self.done.at[at],
            send_sem=self.send.at[i, self.bits + step],
            recv_sem=self.recv.at[i, self.bits + step],
            device_id={"dp": self.me ^ (1 << order[step])},
            device_id_type=MESH,
        )

    def event(self, part, k):
        bits = self.bits
        end, begin = k > self.first, k < self.last
        if end and 0 < k <= bits:
            self.halving(part, k - 1).wait()
            self.add(part, k - 1)
        if end and k > bits:
            self.doubling(part, 2 * bits - k).wait()
        if begin and k < bits:
            self.halving(part, k).start()
        elif begin and k < 2 * bits:
            self.doubling(part, 2 * bits - k - 1).start()

    def due(self, q):
        todo = []
        for k in range(self.first, self.last + 1):
            at = self.polls[min(8, (k * 8 + 2 * self.bits - 1) // (2 * self.bits))]
            if at == q:
                todo += [(self, p, k) for p in self.parts]
        return todo


def greet(dp, flips, other):
    barrier = pltpu.get_barrier_semaphore()
    for flip in flips:
        pl.semaphore_signal(barrier, inc=1, device_id={"dp": dp ^ flip}, device_id_type=MESH)
    pl.semaphore_signal(barrier, inc=1, device_id=other, device_id_type=MESH)
    pl.semaphore_wait(barrier, len(flips) + 1)


def unpack(flat, start, shape, out, sem):
    tiles = shape[0] // 8
    return [
        pltpu.make_async_copy(
            flat.at[start + j * tiles : start + (j + 1) * tiles].reshape(shape[0], 128), out.at[:, j * 128 : (j + 1) * 128], sem.at[j]
        )
        for j in range(shape[1] // 128)
    ]


FFN_POLLS = (
    [6, 10, 12, 14, 16, 18, 20, 22, 24],
    [12, 16, 18, 20, 22, 24, 25],
    [18, 21, 23, 24, 25],
    [24, 25],
)
FFN_LAST = (8, 6, 4, 1)


def ffn(
    bits,
    wout_s, wout_o, gain, shift, back_bias, win_s, bin_s, wback_s, win_o, bin_o, wback_o,
    x, mixed, cot,
    out, gmid, gmix, gout, smalls, gback0, gin0, sums_left,
    mixv, cotv, middle, acc, gacc, n2h, n2l, coth, cotl, hh, hl, ph, plo,
    both, arrived, landed, done, gbin,
    load, store, mp_ss, mp_rs, ss, rs,
):
    i = pl.program_id(0)
    steps = pl.num_programs(0)
    tokens, d = x.shape
    dp = lax.axis_index("dp")
    other = {"mp": 1 - lax.axis_index("mp")}
    theirs, mine = both.at[0], both.at[1]
    groups = both.shape[1]
    sums = [
        Sum(mine.at[j], landed.at[j], done.at[j], ss.at[j], rs.at[j], dp, bits, FFN_POLLS[j], 0, FFN_LAST[j])
        for j in range(groups)
    ]

    def swap(j):
        return pltpu.make_async_remote_copy(
            src_ref=theirs.at[j], dst_ref=arrived.at[j], send_sem=mp_ss.at[j], recv_sem=mp_rs.at[j],
            device_id=other, device_id_type=MESH,
        )

    def join(j):
        swap(j).wait()
        both[1, j] = both[1, j] + arrived[j]

    def poll(q_in_step):
        for step in range(8):
            q = 3 * step + q_in_step
            todo = [e for one in sums for e in one.due(q)]
            if not todo:
                continue

            @pl.when(i == step)
            def _():
                run(todo)

    def run(todo):
        for one, p, k in todo:
            if k == 0 and p is one.parts[0]:
                join(sums.index(one))
            one.event(p, k)

    @pl.when(i == 0)
    def _():
        loads = [
            [
                pltpu.make_async_copy(src.at[t * C : (t + 1) * C], dst.at[t * C : (t + 1) * C], load.at[k, t])
                for k, (src, dst) in enumerate(((x, acc), (mixed, mixv), (cot, cotv)))
            ]
            for t in range(tokens // C)
        ]
        for copies in loads:
            for copy in copies:
                copy.start()
        greet(dp, [1 << b for b in range(bits)], other)
        wo = wout_rows(wout_s, wout_o)
        for t in range(tokens // C):
            for copy in loads[t]:
                copy.wait()
            rows = pl.ds(t * C, C)
            mid = acc[rows, :] + dot3(split(mixv[rows, :]), wo)
            middle[rows, :] = mid
            n, _ = stats(mid)
            n2h[rows, :], n2l[rows, :] = split(n * gain[...] + shift[...])
            coth[rows, :], cotl[rows, :] = split(cotv[rows, :])
            acc[rows, :] = jnp.zeros_like(mid)
            gacc[rows, :] = jnp.zeros_like(mid)

    poll(0)
    bias = jnp.where(i % 2 == 0, bin_s[...], bin_o[...])
    wi = split(jnp.where(i % 2 == 0, win_s[...], win_o[...]))
    wb = split(jnp.where(i % 2 == 0, wback_s[...], wback_o[...]))
    c0 = 0.7978845608028654
    gb = jnp.zeros((1, BH), f32)
    for t in range(tokens // C):
        if t == tokens // C // 2:
            poll(1)
        rows = pl.ds(t * C, C)
        n2 = (n2h[rows, :], n2l[rows, :])
        ct = (coth[rows, :], cotl[rows, :])
        u = dot3(n2, wi) + bias
        gh = dot3(ct, wb, NT)
        u2 = u * u
        th = jnp.tanh(c0 * (u + 0.044715 * (u2 * u)))
        hid = split(0.5 * u * (1.0 + th))
        slope = 0.5 * (1.0 + th) + 0.5 * u * (1.0 - th * th) * (c0 * (1.0 + 0.134145 * u2))
        gp = gh * slope
        gb = gb + jnp.sum(gp, 0, keepdims=True)
        gpre = split(gp)
        hh[rows, :], hl[rows, :] = hid
        ph[rows, :], plo[rows, :] = gpre
        acc[rows, :] = acc[rows, :] + dot3(hid, wb)
        gacc[rows, :] = gacc[rows, :] + dot3(gpre, wi, NT)
    gbin[pl.ds(i, 1), :] = gb
    poll(2)
    j = i // 2
    flat = both.at[i % 2, j]
    for m in range(d // C):
        cols = pl.ds(m * C, C)
        flat_put(flat, m * BH * C // 1024, dot3((hh[...], hl[...]), (coth[:, cols], cotl[:, cols]), TN))
    for m in range(BH // C):
        cols = pl.ds(m * C, C)
        flat_put(flat, d * BH // 1024 + m * d * C // 1024, dot3((n2h[...], n2l[...]), (ph[:, cols], plo[:, cols]), TN))

    @pl.when(i % 2 == 0)
    def _():
        swap(j).start()

    @pl.when(i == steps - 1)
    def _():
        run([e for one in sums for e in one.due(24)])
        wo = wout_rows(wout_s, wout_o)
        gg = jnp.zeros((1, d), f32)
        gs = gg
        gbb = gg
        stores = []
        for t in range(tokens // C):
            rows = pl.ds(t * C, C)
            mid = middle[rows, :]
            ct = cotv[rows, :]
            acc[rows, :] = mid + acc[rows, :] + back_bias[...]
            n, rsq = stats(mid)
            e = gacc[rows, :]
            gg = gg + jnp.sum(e * n, 0, keepdims=True)
            gs = gs + jnp.sum(e, 0, keepdims=True)
            gbb = gbb + jnp.sum(ct, 0, keepdims=True)
            eg = e * gain[...]
            gm = ct + rsq * (eg - jnp.mean(eg, -1, keepdims=True) - n * jnp.mean(eg * n, -1, keepdims=True))
            gacc[rows, :] = gm
            g = split(gm)
            n2h[rows, :], n2l[rows, :] = g
            coth[rows, :], cotl[rows, :] = split(mixv[rows, :])
            mixv[rows, :] = dot3(g, wo, NT)
            for k, (src, dst) in enumerate(((acc, out), (gacc, gmid), (mixv, gmix))):
                stores.append(pltpu.make_async_copy(src.at[t * C : (t + 1) * C], dst.at[t * C : (t + 1) * C], load.at[k, t]))
                stores[-1].start()
        go = dot3((coth[...], cotl[...]), (n2h[...], n2l[...]), TN)
        for slot in range(go.shape[0] // 128):
            flat_put(gout.at[slot % 2], slot // 2 * d // 8, go[slot * 128 : (slot + 1) * 128])
        for parity in range(2):
            smalls[parity, 0:2] = jnp.zeros((2, d), f32)
            smalls[parity, 2:3] = gg
            smalls[parity, 3:4] = gs
            smalls[parity, 4:5] = gbb
            used = groups * BH // d
            for r in range(used):
                per = d // BH
                smalls[parity, 5 + r : 6 + r] = jnp.concatenate(
                    [gbin[2 * (r * per + c) + parity : 2 * (r * per + c) + parity + 1] for c in range(per)], 1
                )
            if used < 3:
                smalls[parity, 5 + used :] = jnp.zeros((3 - used, d), f32)
        last = unpack(done.at[0], 0, (BH, d), gback0, store.at[0:6]) + unpack(
            done.at[0], d * BH // 1024, (d, BH), gin0, store.at[6:12]
        )
        for copy in last:
            copy.start()
        run([e for one in sums for e in one.due(25)])
        for g in range(1, groups):
            left = done if sums[g].last >= bits else both.at[1]
            last.append(pltpu.make_async_copy(left.at[g], sums_left.at[g - 1], store.at[11 + g]))
            last[-1].start()
        for copy in stores + last:
            copy.wait()


POLLS = 4
BWD_POLLS = (
    [0, 0, 0, 0, 0, 0, 0, 3, 5],
    [0, 0, 0, 0, 0, 3, 5, 7, 9],
    [0, 0, 3, 5, 7, 9, 11, 13, 15],
    [3, 5, 7, 9, 11, 13, 15, 16, 16],
    [8, 11, 13, 15, 16, 16, 16, 16, 16],
    None,
)


def small_stages(bits):
    return [(shift, min(2, bits - shift)) for shift in range(0, bits, 2)]


def attn_bwd(
    bits,
    gain, shift, segs, fback, gm, mixed, invt, sq, sk, vv, qfh, qfl, kfh, kfl, ah, al, sp, small,
    x, gmid, w_hi, w_lo, sums_left, gout,
    ginputs, gback1, gin1, gout_out, qkv0, qkv1, smalls,
    n1h, n1l, xv, gv, wh, wl, gh, gl, masks, segc, segr,
    done, ffn, ffn_in, heads, heads_send, heads_mp, heads_in, heads_done, outs, outs_send, outs_mp, outs_in, outs_done,
    sm, sm_in,
    load, store, ss, rs, mp_ss, mp_rs, sm_ss, sm_rs,
):
    slot = pl.program_id(0)
    slots = pl.num_programs(0)
    tokens, d = x.shape
    chunks = tokens // C
    scale = 64.0 ** -0.25
    dp = lax.axis_index("dp")
    other = {"mp": 1 - lax.axis_index("mp")}
    gtiles = gout.shape[1]
    qtiles = d // 8
    left = sums_left.shape[0]
    stages = small_stages(bits)
    polled = [
        Sum(ffn if FFN_LAST[j + 1] * 2 * bits // 8 < bits else None, ffn_in, done.at[j], ss.at[j], rs.at[j], dp, bits,
            BWD_POLLS[j], FFN_LAST[j + 1])
        for j in range(left)
    ]
    outs_sum = Sum(outs, outs_in, outs_done, ss.at[left], rs.at[left], dp, bits, BWD_POLLS[left])
    half_sum, tail_sum = (
        Sum(heads.at[j], heads_in.at[j], heads_done.at[j], ss.at[left + 1 + j], rs.at[left + 1 + j], dp, bits, BWD_POLLS[left + 1 + j])
        for j in range(2)
    )
    polled += [outs_sum, half_sum]

    def to_sibling(src, dst, i):
        return pltpu.make_async_remote_copy(
            src_ref=src, dst_ref=dst, send_sem=mp_ss.at[i], recv_sem=mp_rs.at[i], device_id=other, device_id_type=MESH
        )

    swap_out = to_sibling(outs_send, outs_mp, 0)
    swap_heads = [to_sibling(heads_send.at[j], heads_mp.at[j], 1 + j) for j in range(2)]
    loads = [
        pltpu.make_async_copy(*pair, load.at[i])
        for i, pair in enumerate((
            (x, xv), (gout.at[0], outs_send), (gout.at[1], outs.at[0:gtiles]),
            (w_hi, wh), (w_lo, wl), (gmid, gv),
        ))
    ]
    resumes = [
        pltpu.make_async_copy(sums_left.at[j], done.at[j] if polled[j].total is None else ffn, load.at[6 + j])
        for j in range(left)
    ]

    def run(todo):
        for one, p, k in todo:
            if one is outs_sum and k == 0 and p is one.parts[0]:
                swap_out.wait()
                outs[0:gtiles] = outs[0:gtiles] + outs_mp[...]
            one.event(p, k)

    def due(q):
        return [e for one in polled for e in one.due(q)]

    def poll(q_in_slot):
        for step in range(4):
            todo = due(step * POLLS + q_in_slot)
            if todo:

                @pl.when(slot == step)
                def _():
                    run(todo)

    @pl.when(slot == 0)
    def _():
        for copy in resumes + loads:
            copy.start()
        for copy in resumes:
            copy.wait()
        greet(dp, sorted({1 << b for b in range(bits)} | {j << s for s, w in stages for j in range(1, 1 << w)}), other)
        make_masks(masks, segc, segr, segs)
        for r, used in ((outs, gtiles), (heads.at[0], 3 * qtiles), (heads.at[1], 3 * qtiles)):
            if used < r.shape[0]:
                r[used:] = jnp.zeros((r.shape[0] - used, 8, 128), f32)
        for copy in loads[:3]:
            copy.wait()
        swap_out.start()

    @pl.when(slot == 0)
    def _():
        for c in range(chunks):
            rows = pl.ds(c * C, C)
            n, _ = stats(xv[rows, :])
            n1h[:, rows], n1l[:, rows] = split((n * gain[...] + shift[...]).T)

    lane = lanes(C)
    at = pl.ds(pl.multiple_of(slot * 128, 128), 128)
    keys_one = jnp.where((lane == 64) | (lane == 66), 1.0, 0.0)

    def put(which, rows, g):
        gh[which, rows, at], gl[which, rows, at] = split(g)

    def back(which, rows, grads, feats, s):
        total = None
        sums = []
        for h in range(2):
            dd = grads[h] * (feats[h][0].astype(f32) + feats[h][1].astype(f32))
            sums.append(jnp.sum(dd, -1, keepdims=True))
            for half in split(dd):
                term = dot(half, fback[h], NT)
                total = term if total is None else total + term
        put(which, rows, (fold(total) - s * jnp.where(lane < 64, sums[0], sums[1])) * scale)

    grad = [None, None]
    for c in reversed(range(chunks)):
        poll(chunks - 1 - c)
        rows = pl.ds(c * C, C)
        cont, tailk, carry = seg_flags(segc, segr, c)
        u = gm[rows, :] * invt[rows, :]
        prod = u * mixed[rows, :]
        weights = [-jnp.sum(jnp.where(lane // 64 == h, prod, 0.0), -1, keepdims=True) for h in range(2)]
        ut = u.T
        wt = jnp.where(lane < 64, weights[0], weights[1]).T
        ru = right_pack(u, weights, lane)
        lv = left_pack(vv[rows, :], keys_one, lane)
        gq, gk, gvt, qfs, kfs = [], [], [], [], []
        for h in range(2):
            qf = (qfh[h, rows, :], qfl[h, rows, :])
            kf = (kfh[h, rows, :], kfl[h, rows, :])
            ga = split(dot(ru[h], lv[h], NT) * masks[c])
            gqf = dot3(ga, kf)
            gkf = dot3(ga, qf, TN)
            uth = ut[h * 64 : (h + 1) * 64]
            gvh = dot3(split(uth), (ah[h, rows, :], al[h, rows, :]))
            if c > 0:
                gqf = gqf + cont[0] * dot(ru[h], sp[h, c - 1])
            if c < chunks - 1:
                gkf = gkf + tailk[0] * dot(lv[h], stack_rows(grad[h], (0, 0, 1)))
                gvh = gvh + tailk[1] * dot3(split(grad[h][:64]), kf, NT)
            if c > 0:
                fresh = dot3(split(with_row(uth, wt[h * 64 : h * 64 + 1], 0) * cont[1]), qf)
                grad[h] = fresh if c == chunks - 1 else fresh + carry * grad[h]
            gq.append(gqf)
            gk.append(gkf)
            gvt.append(gvh)
            qfs.append(qf)
            kfs.append(kf)
        back(0, rows, gq, qfs, sq[rows, :])
        back(1, rows, gk, kfs, sk[rows, :])
        put(2, rows, jnp.concatenate(gvt, 0).T)

    def weight_grads(flat):
        g = dot3(
            (n1h[...], n1l[...]), [jnp.concatenate([r[i, :, at] for i in range(3)], 1) for r in (gh, gl)]
        )
        flat_put(flat, 0, g)

    for j in range(2):

        @pl.when(slot == 2 * j)
        def _():
            weight_grads(heads_send.at[j])
            swap_heads[j].start()

    def own_grads(j):
        weight_grads(heads.at[j])
        swap_heads[j].wait()
        used = 3 * qtiles
        heads[j, 0:used] = heads[j, 0:used] + heads_mp[j]

    @pl.when(slot == 1)
    def _():
        own_grads(0)

    @pl.when(slot == slots - 1)
    def _():
        own_grads(1)
        run([(tail_sum, p, 0) for p in tail_sum.parts])
        for copy in loads[3:]:
            copy.wait()
        run([e for one in polled[:left] for e in one.due(16)])
        waiting = [[[e for e in one.due(16) if e[2] == k] for k in range(2 * bits + 1)] for one in polled[left:]]
        waiting = [[e for e in chain if e] for chain in waiting]
        following = [[(tail_sum, p, k) for p in tail_sum.parts] for k in range(1, 2 * bits + 1)]

        def half_next():
            for chain in waiting:
                if chain:
                    run(chain.pop(0))

        def tail_next():
            if following:
                run(following.pop(0))

        stores = []
        for g in range(left):
            stores += unpack(done.at[g], 0, (BH, d), gback1.at[g * BH : (g + 1) * BH], store.at[12 * g : 12 * g + 6])
            stores += unpack(
                done.at[g], d * BH // 1024, (d, BH), gin1.at[:, g * BH : (g + 1) * BH], store.at[12 * g + 6 : 12 * g + 12]
            )
        for copy in stores:
            copy.start()
        half_next()
        gg = jnp.zeros((1, d), f32)
        gs = gg
        for c in range(chunks):
            rows = pl.ds(c * C, C)
            n, rsq = stats(xv[rows, :])
            e = jnp.zeros((C, d), f32)
            for i in range(3):
                e = e + dot3((gh[i, rows, :], gl[i, rows, :]), (wh[i], wl[i]), NT)
            gg = gg + jnp.sum(e * n, 0, keepdims=True)
            gs = gs + jnp.sum(e, 0, keepdims=True)
            eg = e * gain[...]
            gv[rows, :] = gv[rows, :] + rsq * (
                eg - jnp.mean(eg, -1, keepdims=True) - n * jnp.mean(eg * n, -1, keepdims=True)
            )
            tail_next()
            half_next()
        rows_store = [pltpu.make_async_copy(gv, ginputs, store.at[12 * left])]
        rows_store[0].start()
        sm[0] = jnp.concatenate([gg, gs, small[0, 2:]], 0)
        first = to_sibling(sm.at[0], sm_in.at[0], 3)
        first.start()
        tail_next()
        while any(waiting):
            half_next()
        base = 12 * left + 1
        for s in range(gtiles * 8 // d):
            rows_store += unpack(
                outs_done, s * d // 8, (128, d), gout_out.at[s * 128 : (s + 1) * 128], store.at[base + 4 * s : base + 4 * s + 4]
            )
        base += gtiles * 32 // d
        for c in range(3):
            rows_store += unpack(heads_done.at[0], c * qtiles, (d, 128), qkv0.at[c], store.at[base + c : base + c + 1])
        for copy in rows_store[1:]:
            copy.start()
        first.wait()
        sm[1] = jnp.concatenate([gg, gs, small[1, 2:]], 0) + sm_in[0]
        for i, (shift, width) in enumerate(stages):
            digit = (dp >> shift) & ((1 << width) - 1)
            sends = [
                pltpu.make_async_remote_copy(
                    src_ref=sm.at[i + 1], dst_ref=sm_in.at[1 + 4 * i + digit], send_sem=sm_ss.at[3 * i + j - 1],
                    recv_sem=sm_rs.at[3 * i + j - 1], device_id={"dp": dp ^ (j << shift)}, device_id_type=MESH,
                )
                for j in range(1, 1 << width)
            ]
            for copy in sends:
                copy.start()
            sm_in[1 + 4 * i + digit] = sm[i + 1]
            tail_next()
            for copy in sends:
                copy.wait()
            total = sm_in[1 + 4 * i]
            for j in range(1, 1 << width):
                total = total + sm_in[1 + 4 * i + j]
            sm[i + 2] = total
        while following:
            tail_next()
        smalls[...] = sm[len(stages) + 1]
        ends = []
        base += 3
        for c in range(3):
            ends += unpack(heads_done.at[1], c * qtiles, (d, 128), qkv1.at[c], store.at[base + c : base + c + 1])
        for copy in ends:
            copy.start()
        for copy in stores + rows_store + ends:
            copy.wait()


def whole(shape):
    return pl.BlockSpec(shape, lambda i: (0,) * len(shape))


def params(**more):
    return pltpu.CompilerParams(vmem_limit_bytes=VMEM_LIMIT, dimension_semantics=("arbitrary",), **more)


def sds(shape, dtype=f32):
    return jax.ShapeDtypeStruct(shape, dtype)


ANY = pl.BlockSpec(memory_space=pl.ANY)


def run_attn_fwd(x, gain, shift, segs, w, features):
    t, d = x.shape
    heads, _, m = features.shape
    cols = w.shape[2]
    chunks = t // C
    slot = lambda i: (i % 2) * 2 + 1 - i // 2
    per_pair = pl.BlockSpec((t, 128), lambda i: (0, slot(i)))
    per_head = pl.BlockSpec((2, t, m), lambda i: (slot(i), 0, 0))
    sem = lambda *n: pltpu.SemaphoreType.DMA(n)
    return pl.pallas_call(
        attn_fwd,
        grid=(heads,),
        in_specs=[whole((t, d)), whole((1, d)), whole((1, d)), whole(segs.shape), ANY, ANY],
        out_specs=[per_pair] * 3 + [per_head] * 4 + [pl.BlockSpec((2, t, C), lambda i: (slot(i), 0, 0))] * 2
        + [pl.BlockSpec((2, chunks - 1, 256, m), lambda i: (slot(i), 0, 0, 0))] + [per_pair] * 2
        + [pl.BlockSpec((2, 256, m), lambda i: (slot(i), 0, 0))] + [pl.BlockSpec((3, d, 128), lambda i: (0, 0, slot(i)))] * 2,
        out_shape=[sds((t, 2 * cols))] * 3 + [sds((2 * heads, t, m), bf16)] * 4 + [sds((2 * heads, t, C), bf16)] * 2
        + [sds((2 * heads, chunks - 1, 256, m), bf16)] + [sds((t, 2 * cols))] * 2 + [sds((2 * heads, 256, m), bf16)]
        + [sds((3, d, 2 * cols), bf16)] * 2,
        scratch_shapes=[pltpu.VMEM((t, cols), f32)] * 3 + [pltpu.VMEM((t, d), bf16)] * 2 + [pltpu.VMEM((chunks, C, C), f32)]
        + [pltpu.VMEM((t, 128), f32), pltpu.VMEM((1, t), f32)] + [pltpu.VMEM((2,) + w.shape, f32), pltpu.VMEM((2,) + features.shape, f32), sem(2), sem(2), sem(2)],
        cost_estimate=pl.CostEstimate(flops=60 * t * d * d, bytes_accessed=80 * t * d * 4, transcendentals=2 * t * d),
        compiler_params=params(collective_id=3, has_side_effects=True),
        name="attn_fwd",
    )(x, gain, shift, segs, w, features)


def run_ffn(x, mixed, wout_s, wout_o, gain, shift, back_bias, cot, w_s, w_o, dp_size):
    t, d = x.shape
    hid = w_s[0].shape[1]
    cols = mixed.shape[1]
    bits = dp_size.bit_length() - 1
    groups = hid // BH
    tiles = 2 * d * BH // 1024
    weights = [
        pl.BlockSpec((d, BH), lambda i: (0, i // 2)), pl.BlockSpec((1, BH), lambda i: (0, i // 2)),
        pl.BlockSpec((BH, d), lambda i: (i // 2, 0)),
    ]
    half = (2, cols // 2 * d // 1024, 8, 128)
    sem = lambda *n: pltpu.SemaphoreType.DMA(n)
    vm = lambda shape, dtype=f32: pltpu.VMEM(shape, dtype)
    block = (groups, tiles, 8, 128)
    return pl.pallas_call(
        functools.partial(ffn, bits),
        grid=(2 * groups,),
        in_specs=[whole(wout_s.shape), whole(wout_o.shape)] + [whole((1, d))] * 3 + weights * 2 + [ANY] * 3,
        out_specs=[ANY] * 3 + [whole(half), whole((2, 8, d))] + [ANY] * 3,
        out_shape=[sds((t, d)), sds((t, d)), sds((t, cols)), sds(half), sds((2, 8, d)),
                   sds((BH, d)), sds((d, BH)), sds((groups - 1,) + block[1:])],
        scratch_shapes=[vm((t, cols)), vm((t, d)), vm((t, d)), vm((t, d)), vm((t, d))] + [vm((t, d), bf16)] * 4
        + [vm((t, BH), bf16)] * 4
        + [vm((2,) + block), vm(block)] + [vm(block)] * 2 + [vm((2 * groups, BH))]
        + [sem(3, t // C), sem(11 + groups), sem(groups), sem(groups), sem(groups, 3, 2 * bits), sem(groups, 3, 2 * bits)],
        compiler_params=params(collective_id=1, has_side_effects=True),
        name="ffn",
    )(wout_s, wout_o, gain, shift, back_bias, *w_s, *w_o, x, mixed, cot)


def run_attn_bwd(x, gain, shift, segs, gm, saved, small, gmid, sums_left, gout, dp_size):
    sq, sk, vv, qfh, qfl, kfh, kfl, ah, al, sp, mixed, invt, fback, wh, wl = saved
    t, d = x.shape
    heads, _, m = fback.shape
    cols = gm.shape[1]
    chunks = t // C
    bits = dp_size.bit_length() - 1
    up = lambda n: -(-n // dp_size) * dp_size
    stages = len(small_stages(bits))
    tiles = lambda n: pltpu.VMEM((n, 8, 128), f32)
    left, nf = sums_left.shape[:2]
    ng, nq = gout.shape[1], 3 * d // 8
    pair = lambda n: pltpu.VMEM((2, n, 8, 128), f32)
    sem = lambda *n: pltpu.SemaphoreType.DMA(n)
    per_slot = pl.BlockSpec((t, 128), lambda p: (0, p))
    per_head = pl.BlockSpec((2, t, m), lambda p: (p, 0, 0))
    rows = small.shape[1]
    return pl.pallas_call(
        functools.partial(attn_bwd, bits),
        grid=(heads // 2,),
        in_specs=[
            whole((1, d)), whole((1, d)), whole(segs.shape), pl.BlockSpec((2, 256, m), lambda p: (p, 0, 0)),
        ] + [per_slot] * 6 + [per_head] * 4 + [pl.BlockSpec((2, t, C), lambda p: (p, 0, 0))] * 2
        + [pl.BlockSpec((2, chunks - 1, 256, m), lambda p: (p, 0, 0, 0))] + [whole(small.shape)] + [ANY] * 6,
        out_specs=[ANY] * 6 + [whole((rows, d))],
        out_shape=[sds((t, d)), sds((left * BH, d)), sds((d, left * BH)), sds((cols // 2, d)), sds((3, d, 128)), sds((3, d, 128)),
                   sds((rows, d))],
        scratch_shapes=[pltpu.VMEM((d, t), bf16)] * 2 + [pltpu.VMEM((t, d), f32)] * 2 + [pltpu.VMEM((3, d, cols), bf16)] * 2
        + [pltpu.VMEM((3, t, cols), bf16)] * 2 + [pltpu.VMEM((chunks, C, C), f32), pltpu.VMEM((t, 128), f32), pltpu.VMEM((1, t), f32)]
        + [pltpu.VMEM((left, nf, 8, 128), f32), tiles(nf), tiles(nf)] + [pair(up(nq)), pair(nq), pair(nq), pair(up(nq)), pair(up(nq))]
        + [tiles(up(ng)), tiles(ng), tiles(ng), tiles(up(ng)), tiles(up(ng))]
        + [pltpu.VMEM((stages + 2, rows, d), f32), pltpu.VMEM((4 * stages + 1, rows, d), f32)]
        + [sem(6 + left), sem(12 * left + 1 + ng * 32 // d + 6), sem(left + 3, 3, 2 * bits), sem(left + 3, 3, 2 * bits), sem(4), sem(4), sem(3 * stages), sem(3 * stages)],
        compiler_params=params(collective_id=2, has_side_effects=True),
        name="attn_bwd",
    )(gain, shift, segs, fback, gm, mixed, invt, sq, sk, vv, qfh, qfl, kfh, kfl, ah, al, sp, small,
      x, gmid, wh, wl, sums_left, gout)


def place(output, ginputs, gback0, gback1, gin0, gin1, gout, qkv0, qkv1, small, o1, o2, o3, o4, o5, o6, obias, *vectors):
    used = obias.shape[0] // small.shape[1]
    for r in range(used):
        obias[r * small.shape[1] : (r + 1) * small.shape[1]] = small[5 + r]
    for r, vector in enumerate(vectors):
        vector[...] = small[r]
    o1[...] = output[...]
    o2[...] = ginputs[...]
    o4[:, : gin0.shape[1]] = gin0[...]
    o4[:, gin0.shape[1] :] = gin1[...]
    o5[...] = gout[...]
    o6[:, :, :128] = qkv0[...]
    o6[:, :, 128:] = qkv1[...]
    first = pl.program_id(0) * o3.shape[0] < BH

    @pl.when(first)
    def _():
        o3[...] = gback0[...]

    @pl.when(jnp.logical_not(first))
    def _():
        o3[...] = gback1[...]


def run_place(output, ginputs, gback0, gback1, gin0, gin1, gout, qkv0, qkv1, small):
    steps = 4
    back = (gback0.shape[0] + gback1.shape[0], gback0.shape[1])
    ins = (gin0.shape[0], gin0.shape[1] + gin1.shape[1])
    qkv = qkv0.shape[:2] + (2 * qkv0.shape[2],)
    rows = lambda shape: pl.BlockSpec((shape[0] // steps, shape[1]), lambda i: (i, 0))
    mids = lambda shape: pl.BlockSpec((shape[0], shape[1] // steps, shape[2]), lambda i: (0, i, 0))
    size = back[0] // steps
    n0 = gback0.shape[0] // size
    return pl.pallas_call(
        place,
        grid=(steps,),
        in_specs=[
            rows(output.shape), rows(ginputs.shape),
            pl.BlockSpec((size, back[1]), lambda i: (jnp.minimum(i, n0 - 1), 0)),
            pl.BlockSpec((size, back[1]), lambda i: (jnp.maximum(i - n0, 0), 0)),
            rows(gin0.shape), rows(gin1.shape), rows(gout.shape), mids(qkv0.shape), mids(qkv1.shape), whole(small.shape),
        ],
        out_specs=[rows(output.shape), rows(ginputs.shape), rows(back), rows(ins), rows(gout.shape), mids(qkv), whole(back[:1])] + [whole(back[1:])] * 5,
        out_shape=[sds(output.shape), sds(ginputs.shape), sds(back), sds(ins), sds(gout.shape), sds(qkv), sds(back[:1])] + [sds(back[1:])] * 5,
        compiler_params=params(),
        name="place",
    )(output, ginputs, gback0, gback1, gin0, gin1, gout, qkv0, qkv1, small)


def body(
    dp_size,
    inputs, segment_ids, first_gain, first_shift, qkv_weight, out_weight, features,
    second_gain, second_shift, in_weight, in_bias, back_weight, back_bias, cotangent,
):
    swap = [(0, 1), (1, 0)]

    def other(array):
        return lax.ppermute(array, "mp", swap)

    row = lambda v: v.reshape(1, -1)
    out_s = other(out_weight)
    in_s, bin_s, back_s = other(in_weight), other(in_bias), other(back_weight)
    g1, s1, g2, s2 = row(first_gain), row(first_shift), row(second_gain), row(second_shift)
    saved = run_attn_fwd(inputs, g1, s1, segment_ids, qkv_weight, features.swapaxes(1, 2))
    output, gmid, gmix, gout, small, gback0, gin0, sums_left = run_ffn(
        inputs, saved[10], out_s, out_weight, g2, s2, row(back_bias), cotangent,
        (in_s, row(bin_s), back_s), (in_weight, row(in_bias), back_weight), dp_size,
    )
    g_inputs, gback1, gin1, g_out, qkv0, qkv1, small = run_attn_bwd(
        inputs, g1, s1, segment_ids, gmix, saved, small, gmid, sums_left, gout, dp_size,
    )
    output, g_inputs, gback, gin, g_out, gqkv, gbin, *small = run_place(
        output, g_inputs, gback0, gback1, gin0, gin1, g_out, qkv0, qkv1, small
    )
    return (output, g_inputs, small[0], small[1], gqkv, g_out, small[2], small[3], gin, gbin, gback, small[4])


def solution(mesh):
    rows = P(("dp", "mp"), None)
    return jax.shard_map(
        functools.partial(body, mesh.shape["dp"]),
        mesh=mesh,
        in_specs=(
            rows, P("dp", None), P(), P(), P(None, None, "mp"), P("mp", None), P("mp", None, None),
            P(), P(), P(None, "mp"), P("mp"), P("mp", None), P(), rows,
        ),
        out_specs=(
            rows, rows, P(), P(), P(None, None, "mp"), P("mp", None), P(), P(), P(None, "mp"), P("mp"), P("mp", None), P(),
        ),
        check_vma=False,
    )
```
